32 devices in a mesh: section: 2 (over y), seq: 8 (over z, x), mp: 2 (over core).
Axes of the slice: x: 2, y: 2, z: 4, core: 2. Of those that a mesh axis runs over, the one named last changes fastest.
Arguments:
- hidden: bfloat16 [1024, 4096], P('seq'), may hold values from -6 to 6
- hidden_gain: bfloat16 [4096], replicated, may hold values from 0.5 to 1.5
- neighbour_states: bfloat16 [128, 128, 896], P('seq'), may hold values from -6 to 6
- encoder_gain: bfloat16 [896], replicated, may hold values from 0.5 to 1.5
- query_weight: bfloat16 [4096, 2048], P('section', 'mp'), may hold values from -0.09375 to 0.09375
- kv_weight: bfloat16 [2, 896, 2048], P(None, None, 'mp'), may hold values from -0.1875 to 0.1875
- attn_grad: bfloat16 [1024, 2048], P('seq', 'mp'), may hold values from -6 to 6
- neighbour_ids: int32 [16, 16], P('seq'), may hold values from 0 to 15, each once within a row
- valid_counts: int32 [16], P('seq'), may hold values from 2 to 16
Outputs:
- hidden_grad: bfloat16 [1024, 4096], P('seq', ('section', 'mp'))
- query_weight_grad: float32 [4096, 2048], P(('section', 'seq'), 'mp')
- kv_weight_grad: float32 [2, 896, 2048], P(None, ('section', 'seq'), 'mp')
- norm_dot: float32 [1024], P('seq')
The draws below stay inside these ranges and needn't reach their ends.
Inputs may be any that keep to these rules, and one draw needn't show every extreme that they name: `neighbour_ids`: each row lists every one of the 16 pool blocks of its group once.
All inputs are finite; a program needn't handle non-finite values.
Results may differ from the reference program's by a relative error of at most 0.012.
Values may be sent and summed in bfloat16 or wider, within the bound.
No kernel may reach another device: no remote copies, remote signals or barrier semaphores. Data moves between devices by JAX's collectives and lax.ppermute only.
A program may use at most 128 MiB of HBM per device.

```python
import math
import jax
import jax.numpy as jnp
from jax import lax

D = 4096
ENC_W = 896
HEADS = 16
HD = 128
BLOCK = 64
NB_LEN = 128
NB_SLOTS = 16
BLOCK_DEV = 2
TOKENS = 1024
BLOCKS = 16
POOL = 128
N_SEQ = 8


def touch_ends(values, own_key, low, top_value):
    longest = values.shape.index(max(values.shape))
    spots = []
    for shift in (0, 1):
        where = [jax.random.randint(jax.random.fold_in(own_key, axis), (), 0, length) for axis, length in enumerate(values.shape)]
        where[longest] = (where[longest] + shift) % values.shape[longest]
        spots.append(tuple(where))
    return values.at[spots[0]].set(low).at[spots[1]].set(top_value)


def block_levels(own_key, extent, pieces, low, high):
    def one(position, shards_of):
        steps = jax.random.uniform(jax.random.fold_in(jax.random.fold_in(own_key, 6), position), (shards_of,), jnp.float32, low / len(pieces), high / len(pieces))
        return jnp.repeat(jnp.exp(steps), extent[position] // shards_of).reshape((-1,) + (1,) * (len(extent) - position - 1))

    loudness = one(*pieces[0])
    for cut in pieces[1:]:
        loudness = loudness * one(*cut)
    return loudness


def normal_values(stream_key, dims, deviation, limit, shards=(), kind=jnp.bfloat16):
    entries = jax.random.normal(stream_key, dims, jnp.float32) * deviation
    if len(shards) > 0:
        entries = block_levels(stream_key, dims, shards, -0.22, 0.18) * entries
    return jnp.clip(entries, min=-limit, max=limit).astype(kind)


def setup_inputs(seed: int = 0) -> dict:
    splits = jax.random.split(jax.random.key(seed), 10)
    return {
        "hidden": normal_values(splits[0], (TOKENS, D), 1.0, 6.0, ((0, 8),)),
        "hidden_gain": jnp.clip(1.0 + 0.1 * jax.random.normal(splits[1], (D,), jnp.float32), 0.5, 1.5).astype(jnp.bfloat16),
        "neighbour_states": normal_values(splits[2], (POOL, NB_LEN, ENC_W), 1.0, 6.0, ((0, 8),)),
        "encoder_gain": jnp.clip(1.0 + 0.1 * jax.random.normal(splits[3], (ENC_W,), jnp.float32), 0.5, 1.5).astype(jnp.bfloat16),
        "query_weight": normal_values(splits[4], (D, HEADS * HD), D ** -0.5, 0.09375, ((0, 2), (1, 2))),
        "kv_weight": normal_values(splits[5], (2, ENC_W, HEADS * HD), ENC_W ** -0.5, 0.1875, ((2, 2),)),
        "attn_grad": normal_values(splits[6], (TOKENS, HEADS * HD), 1.0, 6.0, ((0, 8), (1, 2))),
        "neighbour_ids": jax.vmap(lambda own: jax.random.permutation(own, NB_SLOTS))(jax.random.split(splits[7], BLOCKS)).reshape((BLOCKS, NB_SLOTS)).astype(jnp.int32),
        "valid_counts": touch_ends(jax.random.randint(splits[8], (BLOCKS,), 2, NB_SLOTS + 1), jax.random.fold_in(splits[8], 1), 2, NB_SLOTS).astype(jnp.int32),
    }


EPSILON = 1e-06

def rms_norm(values, gain_vec):
    widened = values.astype(jnp.float32)
    inv_rms = lax.rsqrt(lax.optimization_barrier(jnp.mean(widened * widened, axis=-1, keepdims=True)) + EPSILON)
    return (widened * inv_rms * gain_vec.astype(jnp.float32), inv_rms)

def block_grads(queries, grad_out, pool_kv, slot_ids, counts):
    block_count, slot_count = slot_ids.shape
    length = pool_kv.shape[2]
    head_count = queries.shape[2]
    head_width = queries.shape[3]
    gathered = pool_kv[:, slot_ids]
    key_rows = gathered[0].reshape(block_count, slot_count * length, head_count, head_width).astype(jnp.float32)
    value_rows = gathered[1].reshape(block_count, slot_count * length, head_count, head_width).astype(jnp.float32)
    query_rows = queries.astype(jnp.float32)
    grad_rows = grad_out.astype(jnp.float32)
    factor = 1.0 / math.sqrt(head_width)
    scores = jnp.einsum('cqhe,ckhe->chqk', query_rows, key_rows) * factor
    slot_of = jnp.arange(slot_count * length, dtype=jnp.int32) // length
    usable = slot_of[None, :] < counts[:, None]
    scores = jnp.where(usable[:, None, None, :], scores, -1e+30)
    attn_probs = jax.nn.softmax(scores, axis=-1)
    grad_probs = jnp.einsum('cqhe,ckhe->chqk', grad_rows, value_rows)
    row_delta = lax.optimization_barrier(jnp.sum(attn_probs * grad_probs, axis=-1, keepdims=True))
    grad_scores = (attn_probs * (grad_probs - row_delta) * factor).astype(jnp.bfloat16).astype(jnp.float32)
    probs_low = attn_probs.astype(jnp.bfloat16).astype(jnp.float32)
    grad_queries = jnp.einsum('chqk,ckhe->cqhe', grad_scores, key_rows)
    grad_keys = jnp.einsum('chqk,cqhe->ckhe', grad_scores, query_rows)
    grad_values = jnp.einsum('chqk,cqhe->ckhe', probs_low, grad_rows)
    pool_size = pool_kv.shape[1]
    onehot = (slot_ids[:, :, None] == jnp.arange(pool_size, dtype=jnp.int32)[None, None, :]).astype(jnp.float32)
    stacked = jnp.stack([grad_keys, grad_values]).reshape(2, block_count, slot_count, length, head_count * head_width)
    pooled = jnp.einsum('csp,kcslf->kplf', onehot, stacked, precision=lax.Precision.HIGHEST)
    return (grad_queries, pooled)

def reference(hidden, hidden_gain, neighbour_states, encoder_gain, query_weight, kv_weight, attn_grad, neighbour_ids, valid_counts):
    all_heads = HEADS * HD
    offset = BLOCK - 1
    normed, inv_rms = rms_norm(hidden, hidden_gain)
    hidden_normed = normed.astype(jnp.bfloat16)
    queries = jnp.dot(hidden_normed, query_weight, preferred_element_type=jnp.float32).astype(jnp.bfloat16)
    padding = jnp.zeros((offset, all_heads), jnp.bfloat16)
    ext_queries = jnp.concatenate([queries[offset:], padding], 0).reshape(N_SEQ, BLOCK_DEV, BLOCK, HEADS, HD)
    ext_grads = jnp.concatenate([attn_grad[offset:], padding], 0).reshape(N_SEQ, BLOCK_DEV, BLOCK, HEADS, HD)
    pool_normed, pool_rms = rms_norm(neighbour_states, encoder_gain)
    pool_low = pool_normed.astype(jnp.bfloat16).reshape(N_SEQ, NB_SLOTS * NB_LEN, ENC_W)
    group_ids = neighbour_ids.reshape(N_SEQ, BLOCK_DEV, NB_SLOTS)
    group_counts = valid_counts.reshape(N_SEQ, BLOCK_DEV)

    def one_group(carry, inputs):
        q_group, g_group, pool_group, ids_group, count_group = inputs
        key_proj = jnp.dot(pool_group, kv_weight[0], preferred_element_type=jnp.float32).astype(jnp.bfloat16)
        value_proj = jnp.dot(pool_group, kv_weight[1], preferred_element_type=jnp.float32).astype(jnp.bfloat16)
        pool_kv = jnp.stack([key_proj, value_proj]).reshape(2, NB_SLOTS, NB_LEN, HEADS, HD)
        grad_queries, pooled = block_grads(q_group, g_group, pool_kv, ids_group, count_group)
        pooled_low = pooled.astype(jnp.bfloat16).reshape(2, NB_SLOTS * NB_LEN, all_heads)
        key_term = jnp.dot(pool_group.T, pooled_low[0], preferred_element_type=jnp.float32)
        value_term = jnp.dot(pool_group.T, pooled_low[1], preferred_element_type=jnp.float32)
        carry = carry + jnp.stack([key_term, value_term])
        return (carry, grad_queries.astype(jnp.bfloat16).reshape(BLOCK_DEV * BLOCK, all_heads))
    kv_weight_grad, ext_dq = lax.scan(one_group, jnp.zeros((2, ENC_W, all_heads), jnp.float32), (ext_queries, ext_grads, pool_low, group_ids, group_counts))
    ext_dq = ext_dq.reshape(TOKENS, all_heads)
    query_grad = jnp.concatenate([padding, ext_dq[:TOKENS - offset]], 0)
    query_weight_grad = jnp.dot(hidden_normed.T, query_grad, preferred_element_type=jnp.float32)
    normed_grad = jnp.dot(query_grad, query_weight.T, preferred_element_type=jnp.float32)
    gain_wide = hidden_gain.astype(jnp.float32)
    hidden_wide = hidden.astype(jnp.float32)
    scaled = gain_wide * normed_grad
    row_dot = lax.optimization_barrier(jnp.sum(scaled * hidden_wide, axis=1, keepdims=True))
    norm_dot = row_dot[:, 0] / math.sqrt(D)
    hidden_grad = (inv_rms * scaled - hidden_wide * inv_rms ** 3 * row_dot / D).astype(jnp.bfloat16)
    return (hidden_grad, query_weight_grad, kv_weight_grad, norm_dot)
```

```python
import functools
import math

import jax
import jax.numpy as jnp
from jax import lax
from jax.experimental import pallas as pl
from jax.experimental.pallas import tpu as pltpu
from jax.sharding import PartitionSpec as P

HD = 128
EPSILON = 1e-06
MASKED = -1e30
VMEM_BYTES = 48 * 1024 * 1024
CHUNKS = 2

F32 = jnp.float32
BF16 = jnp.bfloat16


def shape(dims, kind):
    return jax.ShapeDtypeStruct(dims, kind)


def params():
    return pltpu.CompilerParams(vmem_limit_bytes=VMEM_BYTES)


def cost(flops, moved):
    return pl.CostEstimate(flops=flops, bytes_accessed=moved, transcendentals=0)


def nt_dot(left, right):
    return lax.dot_general(left, right, (((1,), (1,)), ((), ())), preferred_element_type=F32)


def swapped(array, axis, mask):
    size = lax.axis_size(axis)
    return lax.ppermute(array, axis, [(i, i ^ mask) for i in range(size)])


def query_kernel(
    step_count, lead, place, hidden, gain, weight, grad_lead, hn_out, rms_out, keep_out, send_out,
    pair_out, cross_out, total,
):
    step = pl.program_id(0)
    section = place[0]
    width = hidden.shape[1]
    half = width // 2
    depth = weight.shape[0]
    cols = keep_out.shape[1]

    @pl.when(step == 0)
    def _():
        wide = hidden[...].astype(F32)
        inv_rms = lax.rsqrt(jnp.mean(wide * wide, axis=1, keepdims=True) + EPSILON)
        rms_out[...] = inv_rms
        hn_out[...] = (wide * inv_rms * gain[...].astype(F32)).astype(BF16)
        total[...] = jnp.zeros_like(total)

    start = pl.multiple_of(section * half + step * depth, depth)
    total[...] += jnp.dot(hn_out[:, pl.ds(start, depth)], weight[...], preferred_element_type=F32)

    @pl.when(step == step_count - 1)
    def _():
        mine = total[:, pl.ds(pl.multiple_of(section * cols, cols), cols)]
        other = total[:, pl.ds(pl.multiple_of((1 - section) * cols, cols), cols)].astype(BF16)
        keep_out[...] = mine
        send_out[...] = other
        pair_out[0] = mine[:lead].astype(BF16)
        pair_out[1] = grad_lead[...]
        cross_out[...] = other[:lead]


def query_part(place, hidden, gain, weight, attn_grad, lead):
    rows, width = hidden.shape
    half, local = weight.shape
    cols = local // 2
    step_count = 4
    depth = half // step_count
    spec = pltpu.PrefetchScalarGridSpec(
        num_scalar_prefetch=1,
        grid=(step_count,),
        in_specs=[
            pl.BlockSpec((rows, width), lambda k, place: (0, 0)),
            pl.BlockSpec((1, width), lambda k, place: (0, 0)),
            pl.BlockSpec((depth, local), lambda k, place: (k, 0)),
            pl.BlockSpec((lead, cols), lambda k, place: (0, place[0])),
        ],
        out_specs=[
            pl.BlockSpec((rows, width), lambda k, place: (0, 0)),
            pl.BlockSpec((rows, 1), lambda k, place: (0, 0)),
            pl.BlockSpec((rows, cols), lambda k, place: (0, 0)),
            pl.BlockSpec((rows, cols), lambda k, place: (0, 0)),
            pl.BlockSpec((2, lead, cols), lambda k, place: (0, 0, 0)),
            pl.BlockSpec((lead, cols), lambda k, place: (0, 0)),
        ],
        scratch_shapes=[pltpu.VMEM((rows, local), F32)],
    )
    return pl.pallas_call(
        functools.partial(query_kernel, step_count, lead),
        grid_spec=spec,
        out_shape=[
            shape((rows, width), BF16),
            shape((rows, 1), F32),
            shape((rows, cols), F32),
            shape((rows, cols), BF16),
            shape((2, lead, cols), BF16),
            shape((lead, cols), BF16),
        ],
        compiler_params=params(),
        cost_estimate=cost(2 * rows * half * local, 2 * half * local + 4 * rows * width),
        name="query_part",
    )(place, hidden, gain.reshape(1, width), weight, attn_grad)


def columns_kernel(count, place, hn, *rest):
    *outs, turned = rest
    turned[...] = hn[...].T
    half = hn.shape[1] // 2
    span = half // count
    for other in range(count):
        start = (place[1] ^ other) * span
        for part in range(2):
            piece = turned[pl.ds(pl.multiple_of(part * half + start, span), span), :]
            outs[other][part * span : (part + 1) * span, :] = piece


def columns_for(place, hn, count):
    rows, width = hn.shape
    span = width // count
    return pl.pallas_call(
        functools.partial(columns_kernel, count),
        grid_spec=pltpu.PrefetchScalarGridSpec(
            num_scalar_prefetch=1,
            grid=(1,),
            in_specs=[pl.BlockSpec((rows, width), lambda k, place: (0, 0))],
            out_specs=[pl.BlockSpec((span, rows), lambda k, place: (0, 0)) for _ in range(count)],
            scratch_shapes=[pltpu.VMEM((width, rows), BF16)],
        ),
        out_shape=[shape((span, rows), BF16) for _ in range(count)],
        compiler_params=params(),
        cost_estimate=cost(0, 4 * rows * width),
        name="hidden_columns",
    )(place, hn)


def pool_kernel(place, states, gain, weight, kv_out, turned_out):
    wide = states[...].astype(F32)
    inv_rms = lax.rsqrt(jnp.mean(wide * wide, axis=1, keepdims=True) + EPSILON)
    normed = (wide * inv_rms * gain[...].astype(F32)).astype(BF16)
    for which in range(2):
        kv_out[which] = jnp.dot(
            normed, weight[which], preferred_element_type=F32
        ).astype(BF16)
    turned_out[...] = normed.T


def pool_project(place, states, gain, weight):
    rows, width = states.shape
    cols = weight.shape[2] // 2
    block = min(rows, 256)
    return pl.pallas_call(
        pool_kernel,
        grid_spec=pltpu.PrefetchScalarGridSpec(
            num_scalar_prefetch=1,
            grid=(rows // block,),
            in_specs=[
                pl.BlockSpec((block, width), lambda k, place: (k, 0)),
                pl.BlockSpec((1, width), lambda k, place: (0, 0)),
                pl.BlockSpec((2, width, cols), lambda k, place: (0, 0, place[0])),
            ],
            out_specs=[
                pl.BlockSpec((2, block, cols), lambda k, place: (0, k, 0)),
                pl.BlockSpec((width, block), lambda k, place: (0, k)),
            ],
        ),
        out_shape=[shape((2, rows, cols), BF16), shape((width, rows), BF16)],
        compiler_params=params(),
        cost_estimate=cost(4 * rows * width * cols, 4 * rows * width + 8 * rows * cols),
        name="pool_project",
    )(place, states, gain.reshape(1, width), weight)


def rows_at(ref, start, size):
    if size % 8 == 0:
        return ref[pl.ds(pl.multiple_of(start, 8), size), :]
    window = (size + 14) // 8 * 8
    rest = start % 8
    wide = ref[pl.ds(pl.multiple_of(start - rest, 8), window), :]
    return pltpu.roll(wide, window - rest, 0)[:size]


def attend_kernel(
    last, slot_count, count, place, ids, counts, keep, other, pair, cross, grad_own, kv, turned_hbm,
    *rest,
):
    if last:
        before, dq_out, lead_out, *rest = rest
    else:
        dq_out, *rest = rest
    send_out, keep_out, turned, bias, turned_kv, product, sem = rest
    fetch = pltpu.make_async_copy(turned_hbm, turned, sem)
    fetch.start()
    rows, cols = keep.shape
    lead = cross.shape[0]
    keys = kv.shape[1]
    block_count = counts.shape[0]
    block_len = rows // block_count
    offset = block_len - 1
    length = keys // slot_count
    factor = 1.0 / math.sqrt(HD)
    slot_of = lax.broadcasted_iota(jnp.int32, (1, keys), 1) // length
    for block in range(block_count):
        line = jnp.full((1, keys), MASKED, F32)
        for slot in range(slot_count):
            opened = jnp.where(slot < counts[block], ids[block, slot], -1)
            line = jnp.where(slot_of == opened, 0.0, line)
        bias[block * block_len : (block + 1) * block_len, :] = jnp.broadcast_to(
            line, (block_len, keys)
        )
    row = lax.broadcasted_iota(jnp.int32, (rows, 1), 0)
    following = row < offset
    own = keep[...] + other[...].astype(F32)
    led = pair[0].astype(F32) + cross[...].astype(F32)
    padding = jnp.zeros((rows - lead, cols), F32)
    queries = jnp.where(following, jnp.concatenate([led, padding], 0), own)
    queries = pltpu.roll(queries, rows - offset, 0)
    grads = jnp.where(
        following, jnp.concatenate([pair[1].astype(F32), padding], 0), grad_own[...].astype(F32)
    )
    grads = pltpu.roll(grads, rows - offset, 0)
    for head in range(cols // HD):
        span = slice(head * HD, (head + 1) * HD)
        query = queries[:, span].astype(BF16)
        grad = grads[:, span].astype(BF16)
        key = kv[0, :, span]
        value = kv[1, :, span]
        scores = nt_dot(query, key) * factor + bias[...]
        peak = jnp.max(scores, axis=1, keepdims=True)
        weights = jnp.exp(scores - peak)
        norm = 1.0 / jnp.sum(weights, axis=1, keepdims=True)
        probs = weights * norm
        grad_probs = nt_dot(grad, value)
        delta = jnp.sum(probs * grad_probs, axis=1, keepdims=True)
        grad_scores = (probs * (grad_probs - delta) * factor).astype(BF16)
        dq = jnp.dot(grad_scores, key, preferred_element_type=F32)
        dq = pltpu.roll(dq, offset, 0).astype(BF16)
        place_at = before.shape[1] if last else 0
        dq_out[:, place_at + head * HD : place_at + (head + 1) * HD] = dq
        if last:
            lead_out[:, place_at + head * HD : place_at + (head + 1) * HD] = dq[:lead]
        turned_query = queries[:, span].T.astype(BF16)
        turned_grad = grads[:, span].T.astype(BF16)
        turned_kv[span, :] = jnp.dot(
            turned_query, grad_scores, preferred_element_type=F32
        ).astype(BF16)
        turned_kv[cols + head * HD : cols + (head + 1) * HD, :] = jnp.dot(
            turned_grad, probs.astype(BF16), preferred_element_type=F32
        ).astype(BF16)
    if last:
        dq_out[:, : before.shape[1]] = before[...]
        lead_out[:, : before.shape[1]] = before[:lead]
    fetch.wait()
    width = turned.shape[0]
    product[:width] = nt_dot(turned[...], turned_kv[...])
    piece = send_out.shape[2]
    half = width // 2
    for step in range(count):
        for part in range(2):
            for outs, inner in ((keep_out, place[2]), (send_out, 1 - place[2])):
                start = part * half + (2 * (place[1] ^ step) + inner) * piece
                outs[step, part] = rows_at(product, start, piece).astype(outs.dtype)


def attend(
    chunk, place, ids, counts, keep, other, pair, cross, attn_grad, kv, turned, before, seq_size
):
    rows, all_cols = keep.shape
    cols = all_cols // CHUNKS
    lead = cross.shape[0]
    keys = kv.shape[1]
    width = turned.shape[0]
    count = seq_size // 2
    piece = width // (2 * seq_size)
    last = before is not None
    in_specs = [
        pl.BlockSpec((rows, cols), lambda k, place, ids, counts: (0, chunk)),
        pl.BlockSpec((rows, cols), lambda k, place, ids, counts: (0, chunk)),
        pl.BlockSpec((2, lead, cols), lambda k, place, ids, counts: (0, 0, chunk)),
        pl.BlockSpec((lead, cols), lambda k, place, ids, counts: (0, chunk)),
        pl.BlockSpec(
            (rows, cols), lambda k, place, ids, counts: (0, place[0] * CHUNKS + chunk)
        ),
        pl.BlockSpec((2, keys, cols), lambda k, place, ids, counts: (0, 0, chunk)),
        pl.BlockSpec(memory_space=pl.ANY),
    ]
    operands = [keep, other, pair, cross, attn_grad, kv, turned]

    def whole(dims):
        return pl.BlockSpec(dims, lambda k, place, ids, counts: (0,) * len(dims))

    out_shape = []
    if last:
        in_specs.append(whole(before.shape))
        operands.append(before)
        out_shape += [shape((rows, all_cols), BF16), shape((lead, all_cols), BF16)]
    else:
        out_shape.append(shape((rows, cols), BF16))
    out_shape += [
        shape((count, 2, piece, 2 * cols), BF16),
        shape((count, 2, piece, 2 * cols), F32),
    ]
    heads = cols // HD
    return pl.pallas_call(
        functools.partial(attend_kernel, last, ids.shape[1], count),
        grid_spec=pltpu.PrefetchScalarGridSpec(
            num_scalar_prefetch=3,
            grid=(1,),
            in_specs=in_specs,
            out_specs=[whole(out.shape) for out in out_shape],
            scratch_shapes=[
                pltpu.VMEM((width, keys), BF16),
                pltpu.VMEM((rows, keys), F32),
                pltpu.VMEM((2 * cols, keys), BF16),
                pltpu.VMEM((width + 16, 2 * cols), F32),
                pltpu.SemaphoreType.DMA,
            ],
        ),
        out_shape=out_shape,
        compiler_params=params(),
        cost_estimate=cost(
            10 * heads * rows * keys * HD + 4 * width * keys * cols,
            4 * keys * cols + 2 * width * keys + 12 * width * cols,
        ),
        name="attend_%d" % chunk,
    )(place, ids, counts, *operands)


def weight_kernel(count, place, *refs):
    columns, grads, (send_out, keep_out) = refs[:count], refs[count : 2 * count], refs[2 * count :]
    piece = send_out.shape[1]
    for part in range(2):
        for outs, inner in ((send_out, 1 - place[2]), (keep_out, place[2])):
            start = pl.multiple_of((2 * part + inner) * piece, piece)
            total = None
            for column, grad in zip(columns, grads):
                term = jnp.dot(
                    column[pl.ds(start, piece), :], grad[...], preferred_element_type=F32
                )
                total = term if total is None else total + term
            outs[part] = total.astype(outs.dtype)


def weight_part(place, columns, grads):
    count = len(columns)
    span, rows = columns[0].shape
    cols = grads[0].shape[1]
    piece = span // 4

    def whole(dims):
        return pl.BlockSpec(dims, lambda k, place: (0,) * len(dims))

    return pl.pallas_call(
        functools.partial(weight_kernel, count),
        grid_spec=pltpu.PrefetchScalarGridSpec(
            num_scalar_prefetch=1,
            grid=(1,),
            in_specs=[whole((span, rows))] * count + [whole((rows, cols))] * count,
            out_specs=[whole((2, piece, cols)), whole((2, piece, cols))],
        ),
        out_shape=[shape((2, piece, cols), BF16), shape((2, piece, cols), F32)],
        compiler_params=params(),
        cost_estimate=cost(2 * count * span * rows * cols, 6 * span * cols + 2 * count * span * rows),
        name="weight_part",
    )(place, *columns, *grads)


def normed_kernel(step_count, place, own, other, weight, keep_out, send_out, total):
    step = pl.program_id(0)
    cols = own.shape[1]
    depth = weight.shape[0]
    section = place[0]
    first = jnp.where(section == 0, own[...], other[...])
    second = jnp.where(section == 0, other[...], own[...])
    total[step] = nt_dot(first, weight[:, :cols]) + nt_dot(second, weight[:, cols:])

    @pl.when(step == step_count - 1)
    def _():
        per = step_count // 2
        for part in range(per):
            keep_out[:, part * depth : (part + 1) * depth] = total[place[3] * per + part]
            send_out[:, part * depth : (part + 1) * depth] = total[
                (1 - place[3]) * per + part
            ].astype(BF16)


def normed_part(place, own, other, weight):
    rows, cols = own.shape
    half, local = weight.shape
    step_count = 4
    depth = half // step_count
    quarter = half // 2

    def whole(dims):
        return pl.BlockSpec(dims, lambda k, place: (0,) * len(dims))

    return pl.pallas_call(
        functools.partial(normed_kernel, step_count),
        grid_spec=pltpu.PrefetchScalarGridSpec(
            num_scalar_prefetch=1,
            grid=(step_count,),
            in_specs=[
                whole((rows, cols)),
                whole((rows, cols)),
                pl.BlockSpec((depth, local), lambda k, place: (k, 0)),
            ],
            out_specs=[whole((rows, quarter)), whole((rows, quarter))],
            scratch_shapes=[pltpu.VMEM((step_count, rows, depth), F32)],
        ),
        out_shape=[shape((rows, quarter), F32), shape((rows, quarter), BF16)],
        compiler_params=params(),
        cost_estimate=cost(2 * rows * half * local, 2 * half * local + 6 * rows * quarter),
        name="normed_part",
    )(place, own, other, weight)


def body(
    hidden,
    hidden_gain,
    neighbour_states,
    encoder_gain,
    query_weight,
    kv_weight,
    attn_grad,
    neighbour_ids,
    valid_counts,
):
    section = lax.axis_index("section")
    seq = lax.axis_index("seq")
    core = lax.axis_index("mp")
    seq_size = lax.axis_size("seq")
    outer = seq_size // 2
    row_count, model_width = hidden.shape
    half_width, local_cols = query_weight.shape
    cols = local_cols // 2
    slot_total, nb_length, enc_width = neighbour_states.shape
    block_count = neighbour_ids.shape[0]
    block_len = row_count // block_count
    offset = block_len - 1
    place = jnp.stack([section, seq // 2, seq % 2, core]).astype(jnp.int32)

    hn, inv_rms, keep, send, pair, cross = query_part(
        place, hidden, hidden_gain, query_weight, attn_grad, block_len
    )
    other = swapped(send, "section", 1)
    pair_in = lax.ppermute(pair, "seq", [(i, i - 1) for i in range(1, seq_size)])
    cross_in = lax.ppermute(
        cross,
        ("section", "seq"),
        [
            (s * seq_size + i, (1 - s) * seq_size + i - 1)
            for s in range(2)
            for i in range(1, seq_size)
        ],
    )
    columns = columns_for(place, hn, outer)
    columns_in = [columns[0]] + [swapped(columns[d], "seq", 2 * d) for d in range(1, outer)]
    kv, turned = pool_project(
        place, neighbour_states.reshape(slot_total * nb_length, enc_width), encoder_gain, kv_weight
    )

    dq_comb = None
    sums = []
    for chunk in range(CHUNKS):
        *dq_parts, chunk_send, chunk_keep = attend(
            chunk,
            place,
            neighbour_ids,
            valid_counts,
            keep,
            other,
            pair_in,
            cross_in,
            attn_grad,
            kv,
            turned,
            dq_comb,
            seq_size,
        )
        dq_comb = dq_parts[0]
        sums.append((swapped(chunk_send, "seq", 1), chunk_keep))
    dq_lead = dq_parts[1]

    carried = lax.ppermute(dq_lead, "seq", [(i, i + 1) for i in range(seq_size - 1)])
    padded = jnp.concatenate([carried, jnp.zeros((row_count - block_len, cols), BF16)], 0)
    own_dq = jnp.where(jnp.arange(row_count)[:, None] < offset, padded, dq_comb)

    pieces = []
    for received, kept in sums:
        summed = kept + received.astype(F32)
        total = summed[0]
        for d in range(1, outer):
            total = total + swapped(summed[d].astype(BF16), "seq", 2 * d).astype(F32)
        pieces.append(total)
    pieces = jnp.stack(pieces)
    mine = lax.dynamic_index_in_dim(pieces, section, 1, keepdims=False)
    theirs = lax.dynamic_index_in_dim(pieces, 1 - section, 1, keepdims=False)
    got = swapped(theirs.astype(BF16), "section", 1).astype(F32)
    by_section = jnp.where(section == 0, jnp.stack([mine, got]), jnp.stack([got, mine]))
    piece = enc_width // (2 * seq_size)
    kv_grad = by_section.reshape(2, CHUNKS, piece, 2, cols // CHUNKS)
    kv_grad = jnp.transpose(kv_grad, (3, 2, 0, 1, 4)).reshape(2, piece, local_cols)

    dq_other = swapped(own_dq, "section", 1)
    grads_in = [own_dq] + [swapped(own_dq, "seq", 2 * d) for d in range(1, outer)]
    weight_send, weight_keep = weight_part(place, columns_in, grads_in)
    weight_sum = weight_keep + swapped(weight_send, "seq", 1).astype(F32)
    mine = lax.dynamic_index_in_dim(weight_sum, section, 0, keepdims=False)
    theirs = lax.dynamic_index_in_dim(weight_sum, 1 - section, 0, keepdims=False)
    got = swapped(theirs.astype(BF16), "section", 1).astype(F32)
    query_grad = jnp.where(
        section == 0, jnp.concatenate([mine, got], 1), jnp.concatenate([got, mine], 1)
    )

    normed_keep, normed_send = normed_part(place, own_dq, dq_other, query_weight)
    feature_grad = normed_keep + swapped(normed_send, "mp", 1).astype(F32)
    quarter = feature_grad.shape[1]
    start_col = section * half_width + core * quarter
    gain_part = lax.dynamic_slice_in_dim(hidden_gain, start_col, quarter, 0).astype(F32)
    hidden_part = lax.dynamic_slice_in_dim(hidden, start_col, quarter, 1).astype(F32)
    scaled = gain_part * feature_grad
    row_dot = jnp.sum(scaled * hidden_part, axis=1)
    row_dot = row_dot + swapped(row_dot, "mp", 1)
    row_dot = (row_dot + swapped(row_dot, "section", 1))[:, None]
    norm_dot = row_dot[:, 0] / math.sqrt(model_width)
    hidden_grad = (inv_rms * scaled - hidden_part * inv_rms**3 * row_dot / model_width).astype(
        BF16
    )
    return (hidden_grad, query_grad, kv_grad, norm_dot)


def solution(mesh):
    placed = (
        P("seq", None),
        P(),
        P("seq", None, None),
        P(),
        P("section", "mp"),
        P(None, None, "mp"),
        P("seq", "mp"),
        P("seq", None),
        P("seq"),
    )
    return jax.shard_map(
        body,
        mesh=mesh,
        in_specs=placed,
        out_specs=(
            P("seq", ("section", "mp")),
            P(("section", "seq"), "mp"),
            P(None, ("section", "seq"), "mp"),
            P("seq"),
        ),
        check_vma=False,
    )
```

```python
import functools
import math

import jax
import jax.numpy as jnp
from jax import lax
from jax.experimental import pallas as pl
from jax.experimental.pallas import tpu as pltpu
from jax.sharding import PartitionSpec as P

HD = 128
EPSILON = 1e-06
MASKED = -1e30
VMEM_BYTES = 24 * 1024 * 1024
QUERY_VMEM_BYTES = 56 * 1024 * 1024
CHUNKS = 2
FIRST_ATTEND_FLOPS = 20_000_000_000
STEPS = 4

F32 = jnp.float32
BF16 = jnp.bfloat16

IN_VMEM = pl.BlockSpec(memory_space=pltpu.VMEM)
IN_SMEM = pl.BlockSpec(memory_space=pltpu.SMEM)
IN_HBM = pl.BlockSpec(memory_space=pltpu.HBM)


def shape(dims, kind):
    return jax.ShapeDtypeStruct(dims, kind)


def call(
    kernel, name, out_shape, operands, in_specs=None, scratch=(), flops=0, limit=VMEM_BYTES
):
    return pl.pallas_call(
        kernel,
        in_specs=in_specs or [IN_VMEM] * len(operands),
        out_specs=[IN_VMEM] * len(out_shape),
        out_shape=out_shape,
        scratch_shapes=scratch,
        compiler_params=pltpu.CompilerParams(vmem_limit_bytes=limit),
        cost_estimate=pl.CostEstimate(flops=flops, bytes_accessed=0, transcendentals=0),
        name=name,
    )(*operands)


def nt_dot(left, right):
    return lax.dot_general(left, right, (((1,), (1,)), ((), ())), preferred_element_type=F32)


def swapped(array, axis, mask):
    size = lax.axis_size(axis)
    return lax.ppermute(array, axis, [(i, i ^ mask) for i in range(size)])


def after(value, *others):
    return lax.optimization_barrier((value, *others))[0]


def lanes_at(ref, start, size):
    return ref[:, pl.ds(pl.multiple_of(start, size), size)]


def split_column(column):
    high = column.astype(BF16).astype(F32)
    rest = column - high
    middle = rest.astype(BF16).astype(F32)
    low = rest - middle
    lane = lax.broadcasted_iota(jnp.int32, (column.shape[0], HD), 1)
    terms = jnp.where(lane == 0, high, jnp.where(lane == 1, middle, jnp.where(lane == 2, low, 0.0)))
    return terms.astype(BF16)


def joined_column(terms):
    return jnp.sum(terms.astype(F32), axis=1, keepdims=True)


def query_kernel(
    gain, hidden_hbm, weight_hbm, grad_hbm, hn_half, hn_lead, rms_out, keep_out, send_out, pair_out,
    cross_out, hidden_part, gain_part, hidden, hn_out, weight, total, gain_row, sems,
):
    section = lax.axis_index("section")
    core = lax.axis_index("mp")
    rows, width = hidden.shape
    half = width // 2
    quarter = hidden_part.shape[1]
    lead = cross_out.shape[0]
    depth = weight.shape[0] // STEPS
    cols = keep_out.shape[1]
    fetch = pltpu.make_async_copy(hidden_hbm, hidden, sems.at[STEPS])
    fetch.start()
    loads = []
    for step in range(STEPS):
        part = pl.ds(step * depth, depth)
        loads.append(pltpu.make_async_copy(weight_hbm.at[part], weight.at[part], sems.at[step]))
        loads[-1].start()
    grads = pltpu.make_async_copy(
        grad_hbm.at[pl.ds(0, lead), pl.ds(pl.multiple_of(section * cols, cols), cols)],
        pair_out.at[1],
        sems.at[STEPS + 1],
    )
    grads.start()
    gain_row[...] = gain[...].astype(F32).reshape(1, width)
    fetch.wait()
    wide = hidden[...].astype(F32)
    inv_rms = lax.rsqrt(jnp.mean(wide * wide, axis=1, keepdims=True) + EPSILON)
    rms_out[...] = inv_rms
    hn_out[...] = (wide * inv_rms * gain_row[...]).astype(BF16)
    hn_half[...] = lanes_at(hn_out, core * half, half)
    hn_lead[...] = hn_half[:lead]
    own = (2 * section + core) * quarter
    hidden_part[...] = lanes_at(hidden, own, quarter)
    gain_part[...] = lanes_at(gain_row, own, quarter)
    for step in range(STEPS):
        loads[step].wait()
        term = jnp.dot(
            lanes_at(hn_out, section * half + step * depth, depth),
            weight[step * depth : (step + 1) * depth],
            preferred_element_type=F32,
        )
        total[...] = term if step == 0 else total[...] + term
    keep_out[...] = lanes_at(total, section * cols, cols)
    send_out[...] = lanes_at(total, (1 - section) * cols, cols).astype(BF16)
    pair_out[0] = keep_out[:lead].astype(BF16)
    cross_out[...] = send_out[:lead]
    grads.wait()


def query_part(hidden, gain, weight, attn_grad, lead):
    rows, width = hidden.shape
    half, local = weight.shape
    cols = local // 2
    quarter = width // 4
    return call(
        query_kernel,
        "query_part",
        [
            shape((rows, half), BF16),
            shape((lead, half), BF16),
            shape((rows, 1), F32),
            shape((rows, cols), F32),
            shape((rows, cols), BF16),
            shape((2, lead, cols), BF16),
            shape((lead, cols), BF16),
            shape((rows, quarter), BF16),
            shape((1, quarter), F32),
        ],
        [gain, hidden, weight, attn_grad],
        [IN_VMEM, IN_HBM, IN_HBM, IN_HBM],
        [
            pltpu.VMEM((rows, width), BF16),
            pltpu.VMEM((rows, width), BF16),
            pltpu.VMEM((half, local), BF16),
            pltpu.VMEM((rows, local), F32),
            pltpu.VMEM((1, width), F32),
            pltpu.SemaphoreType.DMA((STEPS + 2,)),
        ],
        0,
        QUERY_VMEM_BYTES,
    )


def columns_kernel(count, offset, hn, led, *rest):
    *outs, turned = rest
    lead = led.shape[0]
    follow = lax.broadcasted_iota(jnp.int32, (lead, 1), 0) < offset
    turned[:, :lead] = jnp.where(follow, led[...], hn[:lead]).T
    turned[:, lead:] = hn[lead:].T
    span = outs[0].shape[0]
    outer = lax.axis_index("seq") // 2
    for step in range(count):
        start = pl.multiple_of((outer ^ step) * span, span)
        outs[step][...] = turned[pl.ds(start, span), :]


def columns_for(hn, led, count, offset):
    rows, half = hn.shape
    return call(
        functools.partial(columns_kernel, count, offset),
        "hidden_columns",
        [shape((half // count, rows), BF16)] * count,
        [hn, led],
        None,
        [pltpu.VMEM((half, rows), BF16)],
    )


def pool_kernel(gain, states, weight, kv_out, turned_out):
    rows, width = states.shape
    cols = kv_out.shape[2]
    block = min(rows, 1024)
    start = pl.multiple_of(lax.axis_index("section") * cols, cols)
    gain_row = gain[...].astype(F32).reshape(1, width)
    for base in range(0, rows, block):
        part = slice(base, base + block)
        wide = states[part].astype(F32)
        inv_rms = lax.rsqrt(jnp.mean(wide * wide, axis=1, keepdims=True) + EPSILON)
        normed = (wide * inv_rms * gain_row).astype(BF16)
        for which in range(2):
            kv_out[which, part] = jnp.dot(
                normed, weight[which, :, pl.ds(start, cols)], preferred_element_type=F32
            ).astype(BF16)
        turned_out[:, part] = normed.T


def pool_project(states, gain, weight):
    rows, width = states.shape
    cols = weight.shape[2] // 2
    return call(
        pool_kernel,
        "pool_project",
        [shape((2, rows, cols), BF16), shape((width, rows), BF16)],
        [gain, states, weight],
    )


def rows_at(ref, start, size):
    if size % 8 == 0:
        return ref[pl.ds(pl.multiple_of(start, 8), size), :]
    window = (size + 14) // 8 * 8
    rest = start % 8
    wide = ref[pl.ds(pl.multiple_of(start - rest, 8), window), :]
    return pltpu.roll(wide, window - rest, 0)[:size]


def attend_kernel(
    chunk, slot_count, ids, counts, keep, other, pair, cross, grad_own, kv, *rest
):
    last = chunk == CHUNKS - 1
    if chunk > 0:
        before, dots_before, *rest = rest
    dq_out, dots_out, *rest = rest
    if last:
        lead_out, *rest = rest
    turned_kv, bias = rest
    section = lax.axis_index("section")
    rows, all_cols = keep.shape
    cols = all_cols // CHUNKS
    left = chunk * cols
    here = slice(left, left + cols)
    lead = cross.shape[0]
    keys = kv.shape[1]
    block_count = counts.shape[0]
    block_len = rows // block_count
    offset = block_len - 1
    length = keys // slot_count
    factor = 1.0 / math.sqrt(HD)
    slot_of = lax.broadcasted_iota(jnp.int32, (1, keys), 1) // length
    for block in range(block_count):
        line = jnp.full((1, keys), MASKED, F32)
        for slot in range(slot_count):
            opened = jnp.where(slot < counts[block], ids[block, slot], -1)
            line = jnp.where(slot_of == opened, 0.0, line)
        bias[block * block_len : (block + 1) * block_len, :] = jnp.broadcast_to(
            line, (block_len, keys)
        )
    following = lax.broadcasted_iota(jnp.int32, (rows, 1), 0) < offset
    own = keep[:, here] + other[:, here].astype(F32)
    led = pair[0, :, here].astype(F32) + cross[:, here].astype(F32)
    padding = jnp.zeros((rows - lead, cols), F32)
    queries = jnp.where(following, jnp.concatenate([led, padding], 0), own)
    own = lanes_at(grad_own, section * all_cols + left, cols).astype(F32)
    led = pair[1, :, here].astype(F32)
    grads = jnp.where(following, jnp.concatenate([led, padding], 0), own)
    rolled_queries = pltpu.roll(queries, rows - offset, 0)
    rolled_grads = pltpu.roll(grads, rows - offset, 0)
    dots = dots_before[...] if chunk > 0 else jnp.zeros((rows, 1), F32)
    if chunk > 0:
        dq_out[:, :left] = before[...]
    for head in range(cols // HD):
        span = slice(head * HD, (head + 1) * HD)
        at = slice(left + head * HD, left + (head + 1) * HD)
        query = rolled_queries[:, span].astype(BF16)
        grad = rolled_grads[:, span].astype(BF16)
        key = kv[0, :, at]
        value = kv[1, :, at]
        scores = nt_dot(query, key) * factor + bias[...]
        peak = jnp.max(scores, axis=1, keepdims=True)
        weights = jnp.exp(scores - peak)
        norm = 1.0 / jnp.sum(weights, axis=1, keepdims=True)
        probs = weights * norm
        grad_probs = nt_dot(grad, value)
        delta = jnp.sum(probs * grad_probs, axis=1, keepdims=True)
        grad_scores = (probs * (grad_probs - delta) * factor).astype(BF16)
        dq = jnp.dot(grad_scores, key, preferred_element_type=F32)
        dq = pltpu.roll(dq, offset, 0).astype(BF16)
        dots = dots + jnp.sum(dq.astype(F32) * queries[:, span], axis=1, keepdims=True)
        dq_out[:, at] = dq
        turned_query = rolled_queries[:, span].T.astype(BF16)
        turned_grad = rolled_grads[:, span].T.astype(BF16)
        turned_kv[span, :] = jnp.dot(
            turned_query, grad_scores, preferred_element_type=F32
        ).astype(BF16)
        turned_kv[cols + head * HD : cols + (head + 1) * HD, :] = jnp.dot(
            turned_grad, probs.astype(BF16), preferred_element_type=F32
        ).astype(BF16)
    if last:
        dots_out[...] = split_column(dots)
        lead_out[:, :all_cols] = dq_out[:lead]
        lead_out[:, all_cols:] = dots_out[:lead]
    else:
        dots_out[...] = dots


def kv_part_kernel(count, turned, turned_kv, send_out, keep_out, product):
    outer, inner_own = lax.axis_index("seq") // 2, lax.axis_index("seq") % 2
    width = turned.shape[0]
    product[:width] = nt_dot(turned[...], turned_kv[...])
    piece = send_out.shape[2]
    half = width // 2
    for step in range(count):
        for part in range(2):
            for outs, inner in ((keep_out, inner_own), (send_out, 1 - inner_own)):
                start = part * half + (2 * (outer ^ step) + inner) * piece
                outs[step, part] = rows_at(product, start, piece).astype(outs.dtype)


def attend(chunk, ids, counts, keep, other, pair, cross, attn_grad, kv, before):
    rows, all_cols = keep.shape
    cols = all_cols // CHUNKS
    lead = cross.shape[0]
    keys = kv.shape[1]
    last = chunk == CHUNKS - 1
    operands = [ids, counts, keep, other, pair, cross, attn_grad, kv, *before]
    out_shape = [
        shape((rows, (chunk + 1) * cols), BF16),
        shape((rows, HD), BF16) if last else shape((rows, 1), F32),
    ]
    if last:
        out_shape.append(shape((lead, all_cols + HD), BF16))
    out_shape.append(shape((2 * cols, keys), BF16))
    return call(
        functools.partial(attend_kernel, chunk, ids.shape[1]),
        "attend_%d" % chunk,
        out_shape,
        operands,
        [IN_SMEM] * 2 + [IN_VMEM] * (len(operands) - 2),
        [pltpu.VMEM((rows, keys), F32)],
        0 if last else FIRST_ATTEND_FLOPS,
    )


def kv_part(chunk, turned, turned_kv):
    width = turned.shape[0]
    cols = turned_kv.shape[0]
    seq_size = lax.axis_size("seq")
    count = seq_size // 2
    dims = (count, 2, width // (2 * seq_size), cols)
    return call(
        functools.partial(kv_part_kernel, count),
        "kv_part_%d" % chunk,
        [shape(dims, BF16), shape(dims, F32)],
        [turned, turned_kv],
        None,
        [pltpu.VMEM((width + 16, cols), F32)],
    )


def own_kernel(offset, dq, dots, carried, out):
    lead = carried.shape[0]
    cols = dq.shape[1]
    early = lax.broadcasted_iota(jnp.int32, (lead, 1), 0) < offset
    out[:lead, :cols] = jnp.where(early, carried[:, :cols], dq[:lead])
    out[:lead, cols:] = jnp.where(early, carried[:, cols:], dots[:lead])
    out[lead:, :cols] = dq[lead:]
    out[lead:, cols:] = dots[lead:]


def fold_kernel(kept, received, keep_out, send_out):
    for place in range(keep_out.shape[0]):
        even, odd = 2 * place, 2 * place + 1
        keep_out[place] = kept[even] + received[even].astype(F32)
        send_out[place] = (kept[odd] + received[odd].astype(F32)).astype(BF16)


def fold(kept, received):
    count, *dims = kept.shape
    half = (count // 2, *dims)
    return call(fold_kernel, "fold", [shape(half, F32), shape(half, BF16)], [kept, received])


def outer_kernel(*refs):
    *refs, mine, theirs = refs
    section = lax.axis_index("section")
    for chunk in range(CHUNKS):
        kept, received = refs[2 * chunk : 2 * chunk + 2]
        for out, part in ((mine, section), (theirs, 1 - section)):
            out[chunk] = (kept[0, part] + received[0, part].astype(F32)).astype(out.dtype)


def outer_sums(parts):
    _, _, piece, cols = parts[0].shape
    return call(
        outer_kernel,
        "outer_sums",
        [shape((CHUNKS, piece, cols), F32), shape((CHUNKS, piece, cols), BF16)],
        parts,
    )


def kv_kernel(mine, got, out):
    section = lax.axis_index("section")
    cols = mine.shape[2] // 2
    for chunk in range(CHUNKS):
        for which in range(2):
            for source, part in ((mine, section), (got, 1 - section)):
                start = pl.multiple_of((part * CHUNKS + chunk) * cols, cols)
                out[which, :, pl.ds(start, cols)] = source[
                    chunk, :, which * cols : (which + 1) * cols
                ].astype(F32)


def weight_kernel(order, *refs):
    *refs, send_out, keep_out = refs
    count = len(order)
    mine, theirs, grads = refs[:count], refs[count : 2 * count], refs[2 * count :]
    inner_own = lax.axis_index("seq") % 2
    core = lax.axis_index("mp")
    piece = send_out.shape[1]
    gathered = [ref[index] for ref in grads for index in range(ref.shape[0])]
    for outs, inner in ((send_out, 1 - inner_own), (keep_out, inner_own)):
        rows = pl.ds(pl.multiple_of(inner * piece, piece), piece)
        for part in range(2):
            total = None
            for step, grad in zip(order, gathered):
                column = jnp.where(core == part, mine[step][rows, :], theirs[step][rows, :])
                term = jnp.dot(column, grad, preferred_element_type=F32)
                total = term if total is None else total + term
            outs[part] = total.astype(outs.dtype)


def weight_part(order, mine, theirs, grads):
    span = mine[0].shape[0]
    dims = (2, span // 2, grads[0].shape[2])
    return call(
        functools.partial(weight_kernel, order),
        "weight_part",
        [shape(dims, BF16), shape(dims, F32)],
        [*mine, *theirs, *grads],
    )


def stack_kernel(*refs):
    *refs, out = refs
    start = 0
    for ref in refs:
        out[start : start + ref.shape[0]] = ref[...]
        start += ref.shape[0]


def outer_gather(piece, count, ahead):
    stages, order = [piece], [0]
    bit = count // 2
    while bit:
        whole = stages[0]
        if len(stages) > 1:
            whole = call(
                stack_kernel,
                "stacked",
                [shape((len(order), *piece.shape[1:]), BF16)],
                [after(stages[0], *ahead), *stages[1:]],
            )[0]
        stages.append(swapped(whole, "seq", 2 * bit))
        order += [step ^ bit for step in order]
        bit //= 2
    return stages, order, whole


def weight_sum_kernel(kept, received, mine, theirs):
    section = lax.axis_index("section")
    mine[...] = kept[section] + received[section].astype(F32)
    theirs[...] = (kept[1 - section] + received[1 - section].astype(F32)).astype(BF16)


def side_kernel(mine, got, out):
    section = lax.axis_index("section")
    cols = mine.shape[1]
    out[:, pl.ds(pl.multiple_of(section * cols, cols), cols)] = mine[...]
    out[:, pl.ds(pl.multiple_of((1 - section) * cols, cols), cols)] = got[...].astype(F32)


def normed_kernel(own, other, weight, keep_out, send_out, dots_out, total):
    cols = own.shape[1] - HD
    swap = lax.axis_index("section") == 1
    core = lax.axis_index("mp")
    quarter = keep_out.shape[1]
    first = jnp.where(swap, other[:, :cols], own[:, :cols])
    second = jnp.where(swap, own[:, :cols], other[:, :cols])
    total[...] = nt_dot(first, weight[:, :cols]) + nt_dot(second, weight[:, cols:])
    keep_out[...] = lanes_at(total, core * quarter, quarter)
    send_out[:, :quarter] = lanes_at(total, (1 - core) * quarter, quarter).astype(BF16)
    dots = joined_column(own[:, cols:]) + joined_column(other[:, cols:])
    dots_out[...] = dots
    send_out[:, quarter:] = split_column(dots)


def normed_part(own, other, weight):
    rows = own.shape[0]
    half, local = weight.shape
    quarter = half // 2
    return call(
        normed_kernel,
        "normed_part",
        [shape((rows, quarter), F32), shape((rows, quarter + HD), BF16), shape((rows, 1), F32)],
        [own, other, weight],
        None,
        [pltpu.VMEM((rows, half), F32)],
    )


def hidden_kernel(width, kept, received, dots, hidden, gain, inv_rms, grad_out, dot_out):
    quarter = kept.shape[1]
    inv = inv_rms[...]
    row_dot = (dots[...] + joined_column(received[:, quarter:])) / inv
    wide = jnp.broadcast_to(row_dot * (1.0 / math.sqrt(width)), (row_dot.shape[0], HD))
    dot_out[...] = wide.T[:1]
    scaled = gain[...] * (kept[...] + received[:, :quarter].astype(F32))
    grad_out[...] = (
        inv * scaled - hidden[...].astype(F32) * (inv * inv * inv * row_dot * (1.0 / width))
    ).astype(BF16)


def body(
    hidden,
    hidden_gain,
    neighbour_states,
    encoder_gain,
    query_weight,
    kv_weight,
    attn_grad,
    neighbour_ids,
    valid_counts,
):
    seq_size = lax.axis_size("seq")
    outer = seq_size // 2
    row_count, model_width = hidden.shape
    local_cols = query_weight.shape[1]
    cols = local_cols // 2
    slot_total, nb_length, enc_width = neighbour_states.shape
    block_len = row_count // neighbour_ids.shape[0]
    offset = block_len - 1
    piece = enc_width // (2 * seq_size)
    backward = [(i, i - 1) for i in range(1, seq_size)]

    hn_half, hn_lead, inv_rms, keep, send, pair, cross, hidden_part, gain_part = query_part(
        hidden, hidden_gain, query_weight, attn_grad, block_len
    )
    other = swapped(send, "section", 1)
    pair_in = lax.ppermute(pair, "seq", backward)
    cross_in = lax.ppermute(
        cross,
        ("section", "seq"),
        [(s * seq_size + i, (1 - s) * seq_size + j) for s in range(2) for i, j in backward],
    )
    led = lax.ppermute(hn_lead, "seq", backward)
    kv, turned = pool_project(
        neighbour_states.reshape(slot_total * nb_length, enc_width), encoder_gain, kv_weight
    )

    def attention(chunk, ahead, before):
        return attend(
            chunk, neighbour_ids, valid_counts, after(keep, ahead), other, pair_in, cross_in,
            attn_grad, kv, before,
        )

    def outer_swap(pieces):
        return [swapped(piece, "seq", 2 * (step + 1)) for step, piece in enumerate(pieces)]

    *before, turned_kv = attention(0, turned, ())
    kv_send, kept_first = kv_part(0, turned, turned_kv)
    pair_first = swapped(kv_send, "seq", 1)
    columns = columns_for(hn_half, after(led, kept_first), outer, offset)
    columns_mine = [columns[0]] + outer_swap(columns[1:])
    dq, dots, dq_lead, turned_kv = attention(1, columns[0], before)
    kv_send, kept_second = kv_part(1, turned, turned_kv)
    dq = after(dq, kept_second)
    carried = lax.ppermute(dq_lead, "seq", [(i, i + 1) for i in range(seq_size - 1)])
    pair_second = swapped(kv_send, "seq", 1)
    columns_theirs = [swapped(column, "mp", 1) for column in columns_mine]
    gathered, order, stacked = outer_gather(dq[None], outer, (kept_second, *columns_theirs))

    own_dq = call(
        functools.partial(own_kernel, offset),
        "own_tokens",
        [shape((row_count, cols + HD), BF16)],
        [dq, after(dots, stacked), carried],
    )[0]
    dq_other = swapped(own_dq, "section", 1)

    def fold_on(kept, received, bit, ahead):
        kept, send = fold(after(kept, ahead), received)
        return kept, swapped(send, "seq", 2 * bit), 2 * bit

    def folded(kept, received, bit, ahead):
        while bit < outer:
            kept, received, bit = fold_on(kept, received, bit, ahead)
            ahead = kept
        return kept, received

    first = fold_on(kept_first, pair_first, 1, own_dq) if outer > 1 else (kept_first, pair_first, 1)
    normed_keep, normed_send, normed_dots = normed_part(
        own_dq, after(dq_other, first[0]), query_weight
    )
    normed_in = swapped(normed_send, "mp", 1)
    first = folded(*first, normed_dots)
    second = (kept_second, pair_second, 1)
    if outer > 1:
        second = fold_on(*second, first[0])

    columns_mine[0] = after(columns_mine[0], second[0])
    weight_send, weight_keep = weight_part(order, columns_mine, columns_theirs, gathered)
    weight_in = swapped(weight_send, "seq", 1)

    hidden_grad, norm_dot = call(
        functools.partial(hidden_kernel, model_width),
        "hidden_grad",
        [shape(hidden_part.shape, BF16), shape((1, row_count), F32)],
        [normed_keep, normed_in, after(normed_dots, weight_keep), hidden_part, gain_part, inv_rms],
    )

    second = folded(*second, norm_dot)

    weight_shape = weight_keep.shape[1:]
    mine, theirs = call(
        weight_sum_kernel,
        "weight_sum",
        [shape(weight_shape, F32), shape(weight_shape, BF16)],
        [after(weight_keep, second[0]), weight_in],
    )
    got = swapped(theirs, "section", 1)
    kv_mine, kv_theirs = outer_sums([after(first[0], mine), first[1], *second])
    kv_got = swapped(kv_theirs, "section", 1)

    query_grad = call(
        side_kernel, "query_grad", [shape((weight_shape[0], local_cols), F32)],
        [after(mine, kv_mine), got],
    )[0]
    kv_grad = call(
        kv_kernel, "kv_grad", [shape((2, piece, local_cols), F32)],
        [after(kv_mine, query_grad), kv_got],
    )[0]
    return (hidden_grad, query_grad, kv_grad, norm_dot.reshape(row_count))


def solution(mesh):
    placed = (
        P("seq", None),
        P(),
        P("seq", None, None),
        P(),
        P("section", "mp"),
        P(None, None, "mp"),
        P("seq", "mp"),
        P("seq", None),
        P("seq"),
    )
    return jax.shard_map(
        body,
        mesh=mesh,
        in_specs=placed,
        out_specs=(
            P("seq", ("section", "mp")),
            P(("section", "seq"), "mp"),
            P(None, ("section", "seq"), "mp"),
            P("seq"),
        ),
        check_vma=False,
    )
```

```python
import functools
import math

import jax
import jax.numpy as jnp
from jax import lax
from jax.experimental import pallas as pl
from jax.experimental.pallas import tpu as pltpu
from jax.sharding import PartitionSpec as P

HD = 128
EPSILON = 1e-06
MASKED = -1e30
VMEM_BYTES = 24 * 1024 * 1024
QUERY_VMEM_BYTES = 52 * 1024 * 1024
CHUNKS = 2
STEPS = 4

F32 = jnp.float32
BF16 = jnp.bfloat16

IN_VMEM = pl.BlockSpec(memory_space=pltpu.VMEM)
IN_SMEM = pl.BlockSpec(memory_space=pltpu.SMEM)
IN_HBM = pl.BlockSpec(memory_space=pltpu.HBM)


def shape(dims, kind):
    return jax.ShapeDtypeStruct(dims, kind)


def call(
    kernel, name, out_shape, operands, in_specs=None, scratch=(), flops=0, limit=VMEM_BYTES
):
    return pl.pallas_call(
        kernel,
        in_specs=in_specs or [IN_VMEM] * len(operands),
        out_specs=[IN_VMEM] * len(out_shape),
        out_shape=out_shape,
        scratch_shapes=scratch,
        compiler_params=pltpu.CompilerParams(vmem_limit_bytes=limit),
        cost_estimate=pl.CostEstimate(flops=flops, bytes_accessed=0, transcendentals=0),
        name=name,
    )(*operands)


def nt_dot(left, right):
    return lax.dot_general(left, right, (((1,), (1,)), ((), ())), preferred_element_type=F32)


def swapped(array, axis, mask):
    size = lax.axis_size(axis)
    return lax.ppermute(array, axis, [(i, i ^ mask) for i in range(size)])


def after(value, *others):
    return lax.optimization_barrier((value, *others))[0]


def lanes_at(ref, start, size):
    return ref[:, pl.ds(pl.multiple_of(start, size), size)]


def split_column(column):
    high = column.astype(BF16).astype(F32)
    rest = column - high
    middle = rest.astype(BF16).astype(F32)
    low = rest - middle
    lane = lax.broadcasted_iota(jnp.int32, (column.shape[0], HD), 1)
    terms = jnp.where(lane == 0, high, jnp.where(lane == 1, middle, jnp.where(lane == 2, low, 0.0)))
    return terms.astype(BF16)


def joined_column(terms):
    return jnp.sum(terms.astype(F32), axis=1, keepdims=True)


def query_kernel(
    gain, hidden_hbm, weight_hbm, grad_hbm, hn_half, hn_lead, rms_out, keep_out, send_out, pair_out,
    cross_out, hidden_part, gain_part, hidden, hn_out, weight, total, gain_row, sems,
):
    section = lax.axis_index("section")
    core = lax.axis_index("mp")
    rows, width = hidden.shape
    half = width // 2
    quarter = hidden_part.shape[1]
    lead = cross_out.shape[0]
    depth = weight.shape[0] // STEPS
    cols = keep_out.shape[1]
    fetch = pltpu.make_async_copy(hidden_hbm, hidden, sems.at[STEPS])
    fetch.start()
    loads = []
    for step in range(STEPS):
        part = pl.ds(step * depth, depth)
        loads.append(pltpu.make_async_copy(weight_hbm.at[part], weight.at[part], sems.at[step]))
        loads[-1].start()
    grads = pltpu.make_async_copy(
        grad_hbm.at[pl.ds(0, lead), pl.ds(pl.multiple_of(section * cols, cols), cols)],
        pair_out.at[1],
        sems.at[STEPS + 1],
    )
    grads.start()
    gain_row[...] = gain[...].astype(F32).reshape(1, width)
    fetch.wait()
    wide = hidden[...].astype(F32)
    inv_rms = lax.rsqrt(jnp.mean(wide * wide, axis=1, keepdims=True) + EPSILON)
    rms_out[...] = inv_rms
    hn_out[...] = (wide * inv_rms * gain_row[...]).astype(BF16)
    hn_half[...] = lanes_at(hn_out, core * half, half)
    hn_lead[...] = hn_half[:lead]
    own = (2 * section + core) * quarter
    hidden_part[...] = lanes_at(hidden, own, quarter)
    gain_part[...] = lanes_at(gain_row, own, quarter)
    for step in range(STEPS):
        loads[step].wait()
        term = jnp.dot(
            lanes_at(hn_out, section * half + step * depth, depth),
            weight[step * depth : (step + 1) * depth],
            preferred_element_type=F32,
        )
        total[...] = term if step == 0 else total[...] + term
    keep_out[...] = lanes_at(total, section * cols, cols)
    send_out[...] = lanes_at(total, (1 - section) * cols, cols).astype(BF16)
    pair_out[0] = keep_out[:lead].astype(BF16)
    cross_out[...] = send_out[:lead]
    grads.wait()


def query_part(hidden, gain, weight, attn_grad, lead):
    rows, width = hidden.shape
    half, local = weight.shape
    cols = local // 2
    quarter = width // 4
    return call(
        query_kernel,
        "query_part",
        [
            shape((rows, half), BF16),
            shape((lead, half), BF16),
            shape((rows, 1), F32),
            shape((rows, cols), F32),
            shape((rows, cols), BF16),
            shape((2, lead, cols), BF16),
            shape((lead, cols), BF16),
            shape((rows, quarter), BF16),
            shape((1, quarter), F32),
        ],
        [gain, hidden, weight, attn_grad],
        [IN_VMEM, IN_HBM, IN_HBM, IN_HBM],
        [
            pltpu.VMEM((rows, width), BF16),
            pltpu.VMEM((rows, width), BF16),
            pltpu.VMEM((half, local), BF16),
            pltpu.VMEM((rows, local), F32),
            pltpu.VMEM((1, width), F32),
            pltpu.SemaphoreType.DMA((STEPS + 2,)),
        ],
        0,
        QUERY_VMEM_BYTES,
    )


def columns_kernel(count, offset, hn, led, *rest):
    *outs, turned = rest
    lead = led.shape[0]
    follow = lax.broadcasted_iota(jnp.int32, (lead, 1), 0) < offset
    turned[:, :lead] = jnp.where(follow, led[...], hn[:lead]).T
    turned[:, lead:] = hn[lead:].T
    span = outs[0].shape[0]
    outer = lax.axis_index("seq") // 2
    for step in range(count):
        start = pl.multiple_of((outer ^ step) * span, span)
        outs[step][...] = turned[pl.ds(start, span), :]


def columns_for(hn, led, count, offset):
    rows, half = hn.shape
    return call(
        functools.partial(columns_kernel, count, offset),
        "hidden_columns",
        [shape((half // count, rows), BF16)] * count,
        [hn, led],
        None,
        [pltpu.VMEM((half, rows), BF16)],
    )


def pool_kernel(gain, states, weight, kv_out, turned_out):
    rows, width = states.shape
    cols = kv_out.shape[2]
    block = min(rows, 1024)
    start = pl.multiple_of(lax.axis_index("section") * cols, cols)
    gain_row = gain[...].astype(F32).reshape(1, width)
    for base in range(0, rows, block):
        part = slice(base, base + block)
        wide = states[part].astype(F32)
        inv_rms = lax.rsqrt(jnp.mean(wide * wide, axis=1, keepdims=True) + EPSILON)
        normed = (wide * inv_rms * gain_row).astype(BF16)
        for which in range(2):
            kv_out[which, part] = jnp.dot(
                normed, weight[which, :, pl.ds(start, cols)], preferred_element_type=F32
            ).astype(BF16)
        turned_out[:, part] = normed.T


def pool_project(states, gain, weight):
    rows, width = states.shape
    cols = weight.shape[2] // 2
    return call(
        pool_kernel,
        "pool_project",
        [shape((2, rows, cols), BF16), shape((width, rows), BF16)],
        [gain, states, weight],
    )


def rows_at(ref, start, size):
    if size % 8 == 0:
        return ref[pl.ds(pl.multiple_of(start, 8), size), :]
    window = (size + 14) // 8 * 8
    rest = start % 8
    wide = ref[pl.ds(pl.multiple_of(start - rest, 8), window), :]
    return pltpu.roll(wide, window - rest, 0)[:size]


def attend_kernel(
    chunk, slot_count, ids, counts, keep, other, pair, cross, grad_own, kv, *rest
):
    last = chunk == CHUNKS - 1
    if chunk > 0:
        before, dots_before, *rest = rest
    dq_out, dots_out, *rest = rest
    if last:
        lead_out, *rest = rest
    turned_kv, bias = rest
    section = lax.axis_index("section")
    rows, all_cols = keep.shape
    cols = all_cols // CHUNKS
    left = chunk * cols
    here = slice(left, left + cols)
    lead = cross.shape[0]
    keys = kv.shape[1]
    block_count = counts.shape[0]
    block_len = rows // block_count
    offset = block_len - 1
    length = keys // slot_count
    factor = 1.0 / math.sqrt(HD)
    slot_of = lax.broadcasted_iota(jnp.int32, (1, keys), 1) // length
    for block in range(block_count):
        line = jnp.full((1, keys), MASKED, F32)
        for slot in range(slot_count):
            opened = jnp.where(slot < counts[block], ids[block, slot], -1)
            line = jnp.where(slot_of == opened, 0.0, line)
        bias[block * block_len : (block + 1) * block_len, :] = jnp.broadcast_to(
            line, (block_len, keys)
        )
    following = lax.broadcasted_iota(jnp.int32, (rows, 1), 0) < offset
    own = keep[:, here] + other[:, here].astype(F32)
    led = pair[0, :, here].astype(F32) + cross[:, here].astype(F32)
    padding = jnp.zeros((rows - lead, cols), F32)
    queries = jnp.where(following, jnp.concatenate([led, padding], 0), own)
    own = lanes_at(grad_own, section * all_cols + left, cols).astype(F32)
    led = pair[1, :, here].astype(F32)
    grads = jnp.where(following, jnp.concatenate([led, padding], 0), own)
    rolled_queries = pltpu.roll(queries, rows - offset, 0)
    rolled_grads = pltpu.roll(grads, rows - offset, 0)
    dots = dots_before[...] if chunk > 0 else jnp.zeros((rows, 1), F32)
    if chunk > 0:
        dq_out[:, :left] = before[...]
    for head in range(cols // HD):
        span = slice(head * HD, (head + 1) * HD)
        at = slice(left + head * HD, left + (head + 1) * HD)
        query = rolled_queries[:, span].astype(BF16)
        grad = rolled_grads[:, span].astype(BF16)
        key = kv[0, :, at]
        value = kv[1, :, at]
        scores = nt_dot(query, key) * factor + bias[...]
        peak = jnp.max(scores, axis=1, keepdims=True)
        weights = jnp.exp(scores - peak)
        norm = 1.0 / jnp.sum(weights, axis=1, keepdims=True)
        probs = weights * norm
        grad_probs = nt_dot(grad, value)
        delta = jnp.sum(probs * grad_probs, axis=1, keepdims=True)
        grad_scores = (probs * (grad_probs - delta) * factor).astype(BF16)
        dq = jnp.dot(grad_scores, key, preferred_element_type=F32)
        dq = pltpu.roll(dq, offset, 0).astype(BF16)
        dots = dots + jnp.sum(dq.astype(F32) * queries[:, span], axis=1, keepdims=True)
        dq_out[:, at] = dq
        turned_query = rolled_queries[:, span].T.astype(BF16)
        turned_grad = rolled_grads[:, span].T.astype(BF16)
        turned_kv[span, :] = jnp.dot(
            turned_query, grad_scores, preferred_element_type=F32
        ).astype(BF16)
        turned_kv[cols + head * HD : cols + (head + 1) * HD, :] = jnp.dot(
            turned_grad, probs.astype(BF16), preferred_element_type=F32
        ).astype(BF16)
    if last:
        dots_out[...] = split_column(dots)
        lead_out[:, :all_cols] = dq_out[:lead]
        lead_out[:, all_cols:] = dots_out[:lead]
    else:
        dots_out[...] = dots


def kv_part_kernel(groups, turned, turned_kv, *rest):
    *outs, product = rest
    outer, inner_own = lax.axis_index("seq") // 2, lax.axis_index("seq") % 2
    width = turned.shape[0]
    product[:width] = nt_dot(turned[...], turned_kv[...])
    piece = outs[0].shape[2]
    half = width // 2
    for place, steps in enumerate(groups):
        for index, step in enumerate(steps):
            for part in range(2):
                for out, inner in ((outs[2 * place], 1 - inner_own), (outs[2 * place + 1], inner_own)):
                    start = part * half + (2 * (outer ^ step) + inner) * piece
                    out[index, part] = rows_at(product, start, piece).astype(out.dtype)


def attend(chunk, ids, counts, keep, other, pair, cross, attn_grad, kv, before):
    rows, all_cols = keep.shape
    cols = all_cols // CHUNKS
    lead = cross.shape[0]
    keys = kv.shape[1]
    last = chunk == CHUNKS - 1
    operands = [ids, counts, keep, other, pair, cross, attn_grad, kv, *before]
    out_shape = [
        shape((rows, (chunk + 1) * cols), BF16),
        shape((rows, HD), BF16) if last else shape((rows, 1), F32),
    ]
    if last:
        out_shape.append(shape((lead, all_cols + HD), BF16))
    out_shape.append(shape((2 * cols, keys), BF16))
    return call(
        functools.partial(attend_kernel, chunk, ids.shape[1]),
        "attend_%d" % chunk,
        out_shape,
        operands,
        [IN_SMEM] * 2 + [IN_VMEM] * (len(operands) - 2),
        [pltpu.VMEM((rows, keys), F32)],
    )


def kv_part(chunk, turned, turned_kv, groups):
    width = turned.shape[0]
    cols = turned_kv.shape[0]
    dims = (2, width // (2 * lax.axis_size("seq")), cols)
    return call(
        functools.partial(kv_part_kernel, groups),
        "kv_part_%d" % chunk,
        [shape((len(steps), *dims), kind) for steps in groups for kind in (BF16, F32)],
        [turned, turned_kv],
        None,
        [pltpu.VMEM((width + 16, cols), F32)],
    )


def own_kernel(offset, dq, dots, carried, out):
    lead = carried.shape[0]
    cols = dq.shape[1]
    early = lax.broadcasted_iota(jnp.int32, (lead, 1), 0) < offset
    out[:lead, :cols] = jnp.where(early, carried[:, :cols], dq[:lead])
    out[:lead, cols:] = jnp.where(early, carried[:, cols:], dots[:lead])
    out[lead:, :cols] = dq[lead:]
    out[lead:, cols:] = dots[lead:]


def fold_kernel(kept, received, keep_out, send_out):
    for place in range(keep_out.shape[0]):
        even, odd = 2 * place, 2 * place + 1
        keep_out[place] = kept[even] + received[even].astype(F32)
        send_out[place] = (kept[odd] + received[odd].astype(F32)).astype(BF16)


def fold(kept, received):
    count, *dims = kept.shape
    half = (count // 2, *dims)
    return call(fold_kernel, "fold", [shape(half, F32), shape(half, BF16)], [kept, received])


def add_kernel(kept, received, out):
    out[...] = (kept[...] + received[...].astype(F32)).astype(out.dtype)


def added(kept, received, kind):
    return call(add_kernel, "added", [shape(kept.shape, kind)], [kept, received])[0]


def outer_kernel(*refs):
    *refs, mine, next_out, side_out, cross_out = refs
    section = lax.axis_index("section")
    for chunk in range(CHUNKS):
        kept, received = refs[2 * chunk : 2 * chunk + 2]
        for out, place, part in (
            (next_out, 1, section),
            (cross_out, 1, 1 - section),
            (side_out, 0, 1 - section),
            (mine, 0, section),
        ):
            out[chunk] = (kept[place, part] + received[place, part].astype(F32)).astype(out.dtype)


def outer_sums(parts):
    _, _, piece, cols = parts[0].shape
    dims = (CHUNKS, piece, cols)
    return call(
        outer_kernel, "outer_sums", [shape(dims, F32)] + [shape(dims, BF16)] * 3, parts
    )


def kv_grad_kernel(mine, following, side, cross, out):
    section = lax.axis_index("section")
    cols = mine.shape[2] // 2
    for chunk in range(CHUNKS):
        for which in range(2):
            span = slice(which * cols, (which + 1) * cols)
            own = mine[chunk, :, span] + following[chunk, :, span].astype(F32)
            other = side[chunk, :, span].astype(F32) + cross[chunk, :, span].astype(F32)
            for value, part in ((own, section), (other, 1 - section)):
                start = pl.multiple_of((part * CHUNKS + chunk) * cols, cols)
                out[which, :, pl.ds(start, cols)] = value


def weight_kernel(order, *refs):
    *refs, keep_out, pair_out, side_out, cross_out = refs
    count = len(order)
    mine, theirs, grads = refs[:count], refs[count : 2 * count], refs[2 * count :]
    section = lax.axis_index("section")
    inner_own = lax.axis_index("seq") % 2
    swap = lax.axis_index("mp") != section
    piece = keep_out.shape[0]
    gathered = [ref[index] for ref in grads for index in range(ref.shape[0])]
    for outs, inner, other in (
        (pair_out, 1 - inner_own, False),
        (cross_out, 1 - inner_own, True),
        (side_out, inner_own, True),
        (keep_out, inner_own, False),
    ):
        rows = pl.ds(pl.multiple_of(inner * piece, piece), piece)
        total = None
        for step, grad in zip(order, gathered):
            same, opposite = mine[step][rows, :], theirs[step][rows, :]
            if other:
                same, opposite = opposite, same
            column = jnp.where(swap, opposite, same)
            term = jnp.dot(column, grad, preferred_element_type=F32)
            total = term if total is None else total + term
        outs[...] = total.astype(outs.dtype)


def weight_part(order, mine, theirs, grads):
    dims = (mine[0].shape[0] // 2, grads[0].shape[2])
    return call(
        functools.partial(weight_kernel, order),
        "weight_part",
        [shape(dims, F32)] + [shape(dims, BF16)] * 3,
        [*mine, *theirs, *grads],
    )


def stack_kernel(*refs):
    *refs, out = refs
    start = 0
    for ref in refs:
        out[start : start + ref.shape[0]] = ref[...]
        start += ref.shape[0]


def outer_gather(piece, count, ahead):
    stages, order = [piece], [0]
    bit = count // 2
    while bit:
        whole = stages[0]
        if len(stages) > 1:
            whole = call(
                stack_kernel,
                "stacked",
                [shape((len(order), *piece.shape[1:]), BF16)],
                [after(stages[0], *ahead), *stages[1:]],
            )[0]
        stages.append(swapped(whole, "seq", 2 * bit))
        order += [step ^ bit for step in order]
        bit //= 2
    return stages, order, whole


def query_grad_kernel(kept, paired, side, cross, out):
    section = lax.axis_index("section")
    cols = kept.shape[1]
    own = pl.ds(pl.multiple_of(section * cols, cols), cols)
    out[:, own] = kept[...] + paired[...].astype(F32)
    other = pl.ds(pl.multiple_of((1 - section) * cols, cols), cols)
    out[:, other] = side[...].astype(F32) + cross[...].astype(F32)


def normed_kernel(own, other, weight, keep_out, send_out, more_out, dots_out, total):
    cols = own.shape[1] - HD
    swap = lax.axis_index("section") == 1
    core = lax.axis_index("mp")
    quarter = keep_out.shape[1]
    first = jnp.where(swap, other[:, :cols], own[:, :cols])
    second = jnp.where(swap, own[:, :cols], other[:, :cols])
    total[...] = nt_dot(first, weight[:, :cols]) + nt_dot(second, weight[:, cols:])
    keep_out[...] = lanes_at(total, core * quarter, quarter)
    send = lanes_at(total, (1 - core) * quarter, quarter).astype(BF16)
    send_out[...] = send[:, : quarter // 2]
    more_out[:, : quarter // 2] = send[:, quarter // 2 :]
    dots = joined_column(own[:, cols:]) + joined_column(other[:, cols:])
    dots_out[...] = dots
    more_out[:, quarter // 2 :] = split_column(dots)


def normed_part(own, other, weight):
    rows = own.shape[0]
    half, local = weight.shape
    quarter = half // 2
    return call(
        normed_kernel,
        "normed_part",
        [
            shape((rows, quarter), F32),
            shape((rows, quarter // 2), BF16),
            shape((rows, quarter // 2 + HD), BF16),
            shape((rows, 1), F32),
        ],
        [own, other, weight],
        None,
        [pltpu.VMEM((rows, half), F32)],
    )


def hidden_kernel(width, kept, received, more, dots, hidden, gain, inv_rms, grad_out, dot_out):
    part = received.shape[1]
    inv = inv_rms[...]
    row_dot = (dots[...] + joined_column(more[:, part:])) / inv
    wide = jnp.broadcast_to(row_dot * (1.0 / math.sqrt(width)), (row_dot.shape[0], HD))
    dot_out[...] = wide.T[:1]
    back = inv * inv * inv * row_dot * (1.0 / width)
    for span, ref in ((slice(0, part), received), (slice(part, 2 * part), more)):
        scaled = gain[:, span] * (kept[:, span] + ref[:, :part].astype(F32))
        grad_out[:, span] = (inv * scaled - hidden[:, span].astype(F32) * back).astype(BF16)


def body(
    hidden,
    hidden_gain,
    neighbour_states,
    encoder_gain,
    query_weight,
    kv_weight,
    attn_grad,
    neighbour_ids,
    valid_counts,
):
    seq_size = lax.axis_size("seq")
    outer = seq_size // 2
    row_count, model_width = hidden.shape
    local_cols = query_weight.shape[1]
    cols = local_cols // 2
    slot_total, nb_length, enc_width = neighbour_states.shape
    block_len = row_count // neighbour_ids.shape[0]
    offset = block_len - 1
    piece = enc_width // (2 * seq_size)
    backward = [(i, i - 1) for i in range(1, seq_size)]

    hn_half, hn_lead, inv_rms, keep, send, pair, cross, hidden_part, gain_part = query_part(
        hidden, hidden_gain, query_weight, attn_grad, block_len
    )
    other = swapped(send, "section", 1)
    pair_in = lax.ppermute(pair, "seq", backward)
    cross_in = lax.ppermute(
        cross,
        ("section", "seq"),
        [(s * seq_size + i, (1 - s) * seq_size + j) for s in range(2) for i, j in backward],
    )
    led = lax.ppermute(hn_lead, "seq", backward)
    kv, turned = pool_project(
        neighbour_states.reshape(slot_total * nb_length, enc_width), encoder_gain, kv_weight
    )

    def attention(chunk, ahead, before):
        return attend(
            chunk, neighbour_ids, valid_counts, after(keep, ahead), other, pair_in, cross_in,
            attn_grad, kv, before,
        )

    def outer_swap(pieces):
        return [swapped(piece, "seq", 2 * (step + 1)) for step, piece in enumerate(pieces)]

    def three_ways(pieces, mask):
        near, side, cross = pieces
        pairs = [(s * seq_size + i, (1 - s) * seq_size + (i ^ mask)) for s in range(2) for i in range(seq_size)]
        return (
            swapped(near, "seq", mask),
            swapped(side, "section", 1),
            lax.ppermute(cross, ("section", "seq"), pairs),
        )

    steps = list(range(outer))
    *before, turned_kv = attention(0, turned, ())
    first_send, first_kept = kv_part(0, turned, turned_kv, [steps])
    first_in = swapped(first_send, "seq", 1)
    dq, dots, dq_lead, turned_kv = attention(1, first_kept, before)
    odd_send, odd_kept, even_send, even_kept = kv_part(
        1, turned, turned_kv, [steps[1::2], steps[::2]]
    )
    odd_in = swapped(odd_send, "seq", 1)
    even_in = swapped(even_send, "seq", 1)
    columns = columns_for(hn_half, led, outer, offset)
    columns_mine = [columns[0]] + outer_swap(columns[1:])
    columns_theirs = [swapped(column, "mp", 1) for column in columns_mine]
    carried = lax.ppermute(dq_lead, "seq", [(i, i + 1) for i in range(seq_size - 1)])
    gathered, order, _ = outer_gather(dq[None], outer, ())

    own_dq = call(
        functools.partial(own_kernel, offset),
        "own_tokens",
        [shape((row_count, cols + HD), BF16)],
        [dq, dots, carried],
    )[0]
    dq_other = swapped(own_dq, "section", 1)

    def folded(kept, received, bit):
        while 2 * bit < outer:
            kept, send = fold(kept, received)
            received = swapped(send, "seq", 2 * bit)
            bit *= 2
        return kept, received

    first = folded(after(first_kept, *columns_theirs), first_in, 1)
    odd_sum = added(after(odd_kept, *columns_theirs), odd_in, BF16)
    second = folded(added(even_kept, even_in, F32), swapped(odd_sum, "seq", 2), 2)

    weight_keep, *weight_send = weight_part(order, columns_mine, columns_theirs, gathered)
    weight_in = three_ways(weight_send, 1)

    normed_keep, *normed_send, normed_dots = normed_part(own_dq, dq_other, query_weight)
    normed_in = [swapped(part, "mp", 1) for part in normed_send]
    hidden_grad, norm_dot = call(
        functools.partial(hidden_kernel, model_width),
        "hidden_grad",
        [shape(hidden_part.shape, BF16), shape((1, row_count), F32)],
        [normed_keep, *normed_in, normed_dots, hidden_part, gain_part, inv_rms],
    )

    kv_mine, *kv_send = outer_sums([*first, *second])
    kv_in = three_ways(kv_send, seq_size // 2)

    query_grad = call(
        query_grad_kernel,
        "query_grad",
        [shape((weight_keep.shape[0], local_cols), F32)],
        [weight_keep, *weight_in],
    )[0]
    kv_grad = call(
        kv_grad_kernel,
        "kv_grad",
        [shape((2, piece, local_cols), F32)],
        [kv_mine, *kv_in],
    )[0]
    return (hidden_grad, query_grad, kv_grad, norm_dot.reshape(row_count))


def solution(mesh):
    placed = (
        P("seq", None),
        P(),
        P("seq", None, None),
        P(),
        P("section", "mp"),
        P(None, None, "mp"),
        P("seq", "mp"),
        P("seq", None),
        P("seq"),
    )
    return jax.shard_map(
        body,
        mesh=mesh,
        in_specs=placed,
        out_specs=(
            P("seq", ("section", "mp")),
            P(("section", "seq"), "mp"),
            P(None, ("section", "seq"), "mp"),
            P("seq"),
        ),
        check_vma=False,
    )
```

```python
import functools
import math

import jax
import jax.numpy as jnp
from jax import lax
from jax.experimental import pallas as pl
from jax.experimental.pallas import tpu as pltpu
from jax.sharding import PartitionSpec as P

HD = 128
EPSILON = 1e-06
MASKED = -1e30
VMEM_BYTES = 24 * 1024 * 1024
QUERY_VMEM_BYTES = 52 * 1024 * 1024
CHUNKS = 2
QUERY_FLOPS = 6_000_000_000
FIRST_ATTEND_FLOPS = 4_000_000_000
OUTER_FLOPS = 80_000_000
OWN_FLOPS = 2_000_000_000
STEPS = 4

F32 = jnp.float32
BF16 = jnp.bfloat16

IN_VMEM = pl.BlockSpec(memory_space=pltpu.VMEM)
IN_SMEM = pl.BlockSpec(memory_space=pltpu.SMEM)
IN_HBM = pl.BlockSpec(memory_space=pltpu.HBM)


def shape(dims, kind):
    return jax.ShapeDtypeStruct(dims, kind)


def call(
    kernel, name, out_shape, operands, in_specs=None, scratch=(), flops=0, limit=VMEM_BYTES
):
    return pl.pallas_call(
        kernel,
        in_specs=in_specs or [IN_VMEM] * len(operands),
        out_specs=[IN_VMEM] * len(out_shape),
        out_shape=out_shape,
        scratch_shapes=scratch,
        compiler_params=pltpu.CompilerParams(vmem_limit_bytes=limit),
        cost_estimate=pl.CostEstimate(flops=flops, bytes_accessed=0, transcendentals=0),
        name=name,
    )(*operands)


def nt_dot(left, right):
    return lax.dot_general(left, right, (((1,), (1,)), ((), ())), preferred_element_type=F32)


def swapped(array, axis, mask):
    size = lax.axis_size(axis)
    return lax.ppermute(array, axis, [(i, i ^ mask) for i in range(size)])


def after(value, *others):
    return lax.optimization_barrier((value, *others))[0]


def lanes_at(ref, start, size):
    return ref[:, pl.ds(pl.multiple_of(start, size), size)]


def split_column(column):
    high = column.astype(BF16).astype(F32)
    rest = column - high
    middle = rest.astype(BF16).astype(F32)
    low = rest - middle
    lane = lax.broadcasted_iota(jnp.int32, (column.shape[0], HD), 1)
    terms = jnp.where(lane == 0, high, jnp.where(lane == 1, middle, jnp.where(lane == 2, low, 0.0)))
    return terms.astype(BF16)


def joined_column(terms):
    return jnp.sum(terms.astype(F32), axis=1, keepdims=True)


def query_kernel(
    gain, hidden_hbm, weight_hbm, grad_hbm, hn_half, rms_out, keep_out, send_out, pair_out,
    cross_out, hidden_part, gain_part, hidden, hn_out, weight, total, gain_row, sems,
):
    section = lax.axis_index("section")
    core = lax.axis_index("mp")
    rows, width = hidden.shape
    half = width // 2
    quarter = hidden_part.shape[1]
    lead = cross_out.shape[0]
    depth = weight.shape[0] // STEPS
    cols = keep_out.shape[1]
    fetch = pltpu.make_async_copy(hidden_hbm, hidden, sems.at[STEPS])
    fetch.start()
    loads = []
    for step in range(STEPS):
        part = pl.ds(step * depth, depth)
        loads.append(pltpu.make_async_copy(weight_hbm.at[part], weight.at[part], sems.at[step]))
        loads[-1].start()
    grads = pltpu.make_async_copy(
        grad_hbm.at[pl.ds(0, lead), pl.ds(pl.multiple_of(section * cols, cols), cols)],
        pair_out.at[1],
        sems.at[STEPS + 1],
    )
    grads.start()
    gain_row[...] = gain[...].astype(F32).reshape(1, width)
    fetch.wait()
    wide = hidden[...].astype(F32)
    inv_rms = lax.rsqrt(jnp.mean(wide * wide, axis=1, keepdims=True) + EPSILON)
    rms_out[...] = inv_rms
    hn_out[...] = (wide * inv_rms * gain_row[...]).astype(BF16)
    hn_half[...] = lanes_at(hn_out, core * half, half)
    own = (2 * section + core) * quarter
    hidden_part[...] = lanes_at(hidden, own, quarter)
    gain_part[...] = lanes_at(gain_row, own, quarter)
    for step in range(STEPS):
        loads[step].wait()
        term = jnp.dot(
            lanes_at(hn_out, section * half + step * depth, depth),
            weight[step * depth : (step + 1) * depth],
            preferred_element_type=F32,
        )
        total[...] = term if step == 0 else total[...] + term
    keep_out[...] = lanes_at(total, section * cols, cols)
    send_out[...] = lanes_at(total, (1 - section) * cols, cols).astype(BF16)
    pair_out[0] = keep_out[:lead].astype(BF16)
    cross_out[...] = send_out[:lead]
    grads.wait()


def query_part(hidden, gain, weight, attn_grad, lead):
    rows, width = hidden.shape
    half, local = weight.shape
    cols = local // 2
    quarter = width // 4
    return call(
        query_kernel,
        "query_part",
        [
            shape((rows, half), BF16),
            shape((rows, 1), F32),
            shape((rows, cols), F32),
            shape((rows, cols), BF16),
            shape((2, lead, cols), BF16),
            shape((lead, cols), BF16),
            shape((rows, quarter), BF16),
            shape((1, quarter), F32),
        ],
        [gain, hidden, weight, attn_grad],
        [IN_VMEM, IN_HBM, IN_HBM, IN_HBM],
        [
            pltpu.VMEM((rows, width), BF16),
            pltpu.VMEM((rows, width), BF16),
            pltpu.VMEM((half, local), BF16),
            pltpu.VMEM((rows, local), F32),
            pltpu.VMEM((1, width), F32),
            pltpu.SemaphoreType.DMA((STEPS + 2,)),
        ],
        QUERY_FLOPS,
        QUERY_VMEM_BYTES,
    )


def columns_kernel(hn, keep_out, send_out, turned):
    turned[...] = hn[...].T
    count, span = keep_out.shape[1:3]
    outer = lax.axis_index("seq") // 2
    for out, base in ((keep_out, 0), (send_out, count)):
        for step in range(count):
            start = pl.multiple_of((outer ^ (base + step)) * span, span)
            out[0, step] = turned[pl.ds(start, span), :]


def columns_for(hn, count):
    rows, half = hn.shape
    dims = (1, count // 2, half // count, rows)
    return call(
        columns_kernel,
        "hidden_columns",
        [shape(dims, BF16)] * 2,
        [hn],
        None,
        [pltpu.VMEM((half, rows), BF16)],
    )


def regroup_kernel(kept, received, keep_out, send_out):
    sources = kept.shape[0]
    count = keep_out.shape[1]
    for ref, place in ((kept, 0), (received, sources)):
        keep_out[place : place + sources] = ref[:, :count]
        send_out[place : place + sources] = ref[:, count:]


def columns_exchange(hn, count):
    kept, send = columns_for(hn, count)
    bit = count // 2
    received = swapped(send, "seq", 2 * bit)
    while bit > 1:
        sources, targets, *dims = kept.shape
        dims = (2 * sources, targets // 2, *dims)
        kept, send = call(
            regroup_kernel, "regroup", [shape(dims, BF16)] * 2, [kept, received]
        )
        bit //= 2
        received = swapped(send, "seq", 2 * bit)
    return kept, received


def pool_kernel(gain, states, weight, kv_out, turned_out):
    rows, width = states.shape
    cols = kv_out.shape[2]
    block = min(rows, 1024)
    start = pl.multiple_of(lax.axis_index("section") * cols, cols)
    gain_row = gain[...].astype(F32).reshape(1, width)
    for base in range(0, rows, block):
        part = slice(base, base + block)
        wide = states[part].astype(F32)
        inv_rms = lax.rsqrt(jnp.mean(wide * wide, axis=1, keepdims=True) + EPSILON)
        normed = (wide * inv_rms * gain_row).astype(BF16)
        for which in range(2):
            kv_out[which, part] = jnp.dot(
                normed, weight[which, :, pl.ds(start, cols)], preferred_element_type=F32
            ).astype(BF16)
        turned_out[:, part] = normed.T


def pool_project(states, gain, weight):
    rows, width = states.shape
    cols = weight.shape[2] // 2
    return call(
        pool_kernel,
        "pool_project",
        [shape((2, rows, cols), BF16), shape((width, rows), BF16)],
        [gain, states, weight],
    )


def rows_at(ref, start, size):
    if size % 8 == 0:
        return ref[pl.ds(pl.multiple_of(start, 8), size), :]
    window = (size + 14) // 8 * 8
    rest = start % 8
    wide = ref[pl.ds(pl.multiple_of(start - rest, 8), window), :]
    return pltpu.roll(wide, window - rest, 0)[:size]


def attend_kernel(
    chunk, slot_count, ids, counts, keep, other, pair, cross, grad_own, kv, *rest
):
    last = chunk == CHUNKS - 1
    if chunk > 0:
        before, dots_before, *rest = rest
    dq_out, dots_out, *rest = rest
    if last:
        lead_out, *rest = rest
    turned_kv, bias = rest
    section = lax.axis_index("section")
    rows, all_cols = keep.shape
    cols = all_cols // CHUNKS
    left = chunk * cols
    here = slice(left, left + cols)
    lead = cross.shape[0]
    keys = kv.shape[1]
    block_count = counts.shape[0]
    block_len = rows // block_count
    offset = block_len - 1
    length = keys // slot_count
    factor = 1.0 / math.sqrt(HD)
    slot_of = lax.broadcasted_iota(jnp.int32, (1, keys), 1) // length
    for block in range(block_count):
        line = jnp.full((1, keys), MASKED, F32)
        for slot in range(slot_count):
            opened = jnp.where(slot < counts[block], ids[block, slot], -1)
            line = jnp.where(slot_of == opened, 0.0, line)
        bias[block * block_len : (block + 1) * block_len, :] = jnp.broadcast_to(
            line, (block_len, keys)
        )
    following = lax.broadcasted_iota(jnp.int32, (rows, 1), 0) < offset
    own = keep[:, here] + other[:, here].astype(F32)
    led = pair[0, :, here].astype(F32) + cross[:, here].astype(F32)
    padding = jnp.zeros((rows - lead, cols), F32)
    queries = jnp.where(following, jnp.concatenate([led, padding], 0), own)
    own = lanes_at(grad_own, section * all_cols + left, cols).astype(F32)
    led = pair[1, :, here].astype(F32)
    grads = jnp.where(following, jnp.concatenate([led, padding], 0), own)
    rolled_queries = pltpu.roll(queries, rows - offset, 0)
    rolled_grads = pltpu.roll(grads, rows - offset, 0)
    dots = dots_before[...] if chunk > 0 else jnp.zeros((rows, 1), F32)
    if chunk > 0:
        dq_out[:, :left] = before[...]
    for head in range(cols // HD):
        span = slice(head * HD, (head + 1) * HD)
        at = slice(left + head * HD, left + (head + 1) * HD)
        query = rolled_queries[:, span].astype(BF16)
        grad = rolled_grads[:, span].astype(BF16)
        key = kv[0, :, at]
        value = kv[1, :, at]
        scores = nt_dot(query, key) * factor + bias[...]
        peak = jnp.max(scores, axis=1, keepdims=True)
        weights = jnp.exp(scores - peak)
        norm = 1.0 / jnp.sum(weights, axis=1, keepdims=True)
        probs = weights * norm
        grad_probs = nt_dot(grad, value)
        delta = jnp.sum(probs * grad_probs, axis=1, keepdims=True)
        grad_scores = (probs * (grad_probs - delta) * factor).astype(BF16)
        dq = jnp.dot(grad_scores, key, preferred_element_type=F32)
        dq = pltpu.roll(dq, offset, 0).astype(BF16)
        dots = dots + jnp.sum(dq.astype(F32) * queries[:, span], axis=1, keepdims=True)
        dq_out[:, at] = dq
        turned_query = rolled_queries[:, span].T.astype(BF16)
        turned_grad = rolled_grads[:, span].T.astype(BF16)
        turned_kv[span, :] = jnp.dot(
            turned_query, grad_scores, preferred_element_type=F32
        ).astype(BF16)
        turned_kv[cols + head * HD : cols + (head + 1) * HD, :] = jnp.dot(
            turned_grad, probs.astype(BF16), preferred_element_type=F32
        ).astype(BF16)
    if last:
        dots_out[...] = split_column(dots)
        lead_out[:, :all_cols] = dq_out[:lead]
        lead_out[:, all_cols:] = dots_out[:lead]
    else:
        dots_out[...] = dots


def kv_part_kernel(groups, turned, turned_kv, *rest):
    *outs, product = rest
    outer, inner_own = lax.axis_index("seq") // 2, lax.axis_index("seq") % 2
    width = turned.shape[0]
    product[:width] = nt_dot(turned[...], turned_kv[...])
    piece = outs[0].shape[2]
    half = width // 2
    for place, steps in enumerate(groups):
        for index, step in enumerate(steps):
            for part in range(2):
                for out, inner in ((outs[2 * place], 1 - inner_own), (outs[2 * place + 1], inner_own)):
                    start = part * half + (2 * (outer ^ step) + inner) * piece
                    out[index, part] = rows_at(product, start, piece).astype(out.dtype)


def attend(chunk, ids, counts, keep, other, pair, cross, attn_grad, kv, before):
    rows, all_cols = keep.shape
    cols = all_cols // CHUNKS
    lead = cross.shape[0]
    keys = kv.shape[1]
    last = chunk == CHUNKS - 1
    operands = [ids, counts, keep, other, pair, cross, attn_grad, kv, *before]
    out_shape = [
        shape((rows, (chunk + 1) * cols), BF16),
        shape((rows, HD), BF16) if last else shape((rows, 1), F32),
    ]
    if last:
        out_shape.append(shape((lead, all_cols + HD), BF16))
    out_shape.append(shape((2 * cols, keys), BF16))
    return call(
        functools.partial(attend_kernel, chunk, ids.shape[1]),
        "attend_%d" % chunk,
        out_shape,
        operands,
        [IN_SMEM] * 2 + [IN_VMEM] * (len(operands) - 2),
        [pltpu.VMEM((rows, keys), F32)],
        0 if last else FIRST_ATTEND_FLOPS,
    )


def kv_part(chunk, turned, turned_kv, groups):
    width = turned.shape[0]
    cols = turned_kv.shape[0]
    dims = (2, width // (2 * lax.axis_size("seq")), cols)
    return call(
        functools.partial(kv_part_kernel, groups),
        "kv_part_%d" % chunk,
        [shape((len(steps), *dims), kind) for steps in groups for kind in (BF16, F32)],
        [turned, turned_kv],
        None,
        [pltpu.VMEM((width + 16, cols), F32)],
    )


def own_kernel(offset, dq, dots, carried, out, grads_out):
    lead = carried.shape[0]
    cols = dq.shape[1]
    early = lax.broadcasted_iota(jnp.int32, (lead, 1), 0) < offset
    out[:lead, :cols] = jnp.where(early, carried[:, :cols], dq[:lead])
    out[:lead, cols:] = jnp.where(early, carried[:, cols:], dots[:lead])
    out[lead:, :cols] = dq[lead:]
    out[lead:, cols:] = dots[lead:]
    grads_out[0] = out[:, :cols]


def fold_kernel(kept, received, keep_out, send_out):
    for place in range(keep_out.shape[0]):
        even, odd = 2 * place, 2 * place + 1
        keep_out[place] = kept[even] + received[even].astype(F32)
        send_out[place] = (kept[odd] + received[odd].astype(F32)).astype(BF16)


def fold(kept, received):
    count, *dims = kept.shape
    half = (count // 2, *dims)
    return call(fold_kernel, "fold", [shape(half, F32), shape(half, BF16)], [kept, received])


def add_kernel(kept, received, out):
    out[...] = (kept[...] + received[...].astype(F32)).astype(out.dtype)


def added(kept, received, kind):
    return call(add_kernel, "added", [shape(kept.shape, kind)], [kept, received])[0]


def outer_kernel(*refs):
    *refs, mine, next_out, side_out, cross_out = refs
    section = lax.axis_index("section")
    for chunk in range(CHUNKS):
        kept, received = refs[2 * chunk : 2 * chunk + 2]
        for out, place, part in (
            (next_out, 1, section),
            (cross_out, 1, 1 - section),
            (side_out, 0, 1 - section),
            (mine, 0, section),
        ):
            out[chunk] = (kept[place, part] + received[place, part].astype(F32)).astype(out.dtype)


def outer_sums(parts):
    _, _, piece, cols = parts[0].shape
    dims = (CHUNKS, piece, cols)
    return call(
        outer_kernel, "outer_sums", [shape(dims, F32)] + [shape(dims, BF16)] * 3, parts,
        flops=OUTER_FLOPS,
    )


def kv_grad_kernel(mine, following, side, cross, out):
    section = lax.axis_index("section")
    cols = mine.shape[2] // 2
    for chunk in range(CHUNKS):
        for which in range(2):
            span = slice(which * cols, (which + 1) * cols)
            own = mine[chunk, :, span] + following[chunk, :, span].astype(F32)
            other = side[chunk, :, span].astype(F32) + cross[chunk, :, span].astype(F32)
            for value, part in ((own, section), (other, 1 - section)):
                start = pl.multiple_of((part * CHUNKS + chunk) * cols, cols)
                out[which, :, pl.ds(start, cols)] = value


def weight_kernel(*refs):
    *refs, keep_out, pair_out, side_out, cross_out = refs
    mine, theirs, grads = refs[:2], refs[2:4], refs[4:]
    section = lax.axis_index("section")
    inner_own = lax.axis_index("seq") % 2
    swap = lax.axis_index("mp") != section
    piece = keep_out.shape[0]
    gathered = [ref[index] for ref in grads for index in range(ref.shape[0])]
    half = len(gathered) // 2
    for outs, inner, other in (
        (pair_out, 1 - inner_own, False),
        (cross_out, 1 - inner_own, True),
        (side_out, inner_own, True),
        (keep_out, inner_own, False),
    ):
        rows = pl.ds(pl.multiple_of(inner * piece, piece), piece)
        total = None
        for place, grad in enumerate(gathered):
            same, opposite = (refs[place // half][place % half, 0, rows, :] for refs in (mine, theirs))
            if other:
                same, opposite = opposite, same
            column = jnp.where(swap, opposite, same)
            term = jnp.dot(column, grad, preferred_element_type=F32)
            total = term if total is None else total + term
        outs[...] = total.astype(outs.dtype)


def weight_part(mine, theirs, grads):
    dims = (mine[0].shape[2] // 2, grads[0].shape[2])
    return call(
        weight_kernel,
        "weight_part",
        [shape(dims, F32)] + [shape(dims, BF16)] * 3,
        [*mine, *theirs, *grads],
    )


def stack_kernel(*refs):
    *refs, out = refs
    start = 0
    for ref in refs:
        out[start : start + ref.shape[0]] = ref[...]
        start += ref.shape[0]


def outer_gather(piece, count, ahead):
    stages, whole = [piece], piece
    bit = count // 2
    while bit:
        if len(stages) > 1:
            whole = call(
                stack_kernel,
                "stacked",
                [shape((2 * whole.shape[0], *piece.shape[1:]), BF16)],
                [after(stages[0], *ahead), *stages[1:]],
            )[0]
        stages.append(swapped(whole, "seq", 2 * bit))
        bit //= 2
    return stages


def query_grad_kernel(kept, paired, side, cross, out):
    section = lax.axis_index("section")
    cols = kept.shape[1]
    own = pl.ds(pl.multiple_of(section * cols, cols), cols)
    out[:, own] = kept[...] + paired[...].astype(F32)
    other = pl.ds(pl.multiple_of((1 - section) * cols, cols), cols)
    out[:, other] = side[...].astype(F32) + cross[...].astype(F32)


def normed_kernel(own, other, weight, keep_out, dots_out, send_out, total):
    cols = own.shape[1] - HD
    swap = lax.axis_index("section") == 1
    core = lax.axis_index("mp")
    quarter = keep_out.shape[1]
    first = jnp.where(swap, other[:, :cols], own[:, :cols])
    second = jnp.where(swap, own[:, :cols], other[:, :cols])
    total[...] = nt_dot(first, weight[:, :cols]) + nt_dot(second, weight[:, cols:])
    keep_out[...] = lanes_at(total, core * quarter, quarter)
    send_out[:, :quarter] = lanes_at(total, (1 - core) * quarter, quarter).astype(BF16)
    dots = joined_column(own[:, cols:]) + joined_column(other[:, cols:])
    dots_out[...] = dots
    send_out[:, quarter:] = split_column(dots)


def normed_part(own, other, weight):
    rows = own.shape[0]
    half = weight.shape[0]
    quarter = half // 2
    return call(
        normed_kernel,
        "normed_part",
        [shape((rows, quarter), F32), shape((rows, 1), F32), shape((rows, quarter + HD), BF16)],
        [own, other, weight],
        None,
        [pltpu.VMEM((rows, half), F32)],
    )


def hidden_kernel(width, kept, received, dots, hidden, gain, inv_rms, grad_out, dot_out):
    quarter = kept.shape[1]
    inv = inv_rms[...]
    row_dot = (dots[...] + joined_column(received[:, quarter:])) / inv
    wide = jnp.broadcast_to(row_dot * (1.0 / math.sqrt(width)), (row_dot.shape[0], HD))
    dot_out[...] = wide.T[:1]
    scaled = gain[...] * (kept[...] + received[:, :quarter].astype(F32))
    grad_out[...] = (
        inv * scaled - hidden[...].astype(F32) * (inv * inv * inv * row_dot * (1.0 / width))
    ).astype(BF16)


def body(
    hidden,
    hidden_gain,
    neighbour_states,
    encoder_gain,
    query_weight,
    kv_weight,
    attn_grad,
    neighbour_ids,
    valid_counts,
):
    seq_size = lax.axis_size("seq")
    outer = seq_size // 2
    row_count, model_width = hidden.shape
    local_cols = query_weight.shape[1]
    cols = local_cols // 2
    slot_total, nb_length, enc_width = neighbour_states.shape
    block_len = row_count // neighbour_ids.shape[0]
    offset = block_len - 1
    piece = enc_width // (2 * seq_size)
    backward = [(i, i - 1) for i in range(1, seq_size)]

    hn_half, inv_rms, keep, send, pair, cross, hidden_part, gain_part = query_part(
        hidden, hidden_gain, query_weight, attn_grad, block_len
    )
    other = swapped(send, "section", 1)
    pair_in = lax.ppermute(pair, "seq", backward)
    cross_in = lax.ppermute(
        cross,
        ("section", "seq"),
        [(s * seq_size + i, (1 - s) * seq_size + j) for s in range(2) for i, j in backward],
    )
    kv, turned = pool_project(
        neighbour_states.reshape(slot_total * nb_length, enc_width), encoder_gain, kv_weight
    )

    def attention(chunk, ahead, before):
        return attend(
            chunk, neighbour_ids, valid_counts, after(keep, ahead), other, pair_in, cross_in,
            attn_grad, kv, before,
        )

    def three_ways(pieces, mask):
        near, side, cross = pieces
        pairs = [(s * seq_size + i, (1 - s) * seq_size + (i ^ mask)) for s in range(2) for i in range(seq_size)]
        return (
            swapped(near, "seq", mask),
            swapped(side, "section", 1),
            lax.ppermute(cross, ("section", "seq"), pairs),
        )

    columns_mine = columns_exchange(after(hn_half, turned), outer)
    columns_theirs = [swapped(column, "mp", 1) for column in columns_mine]

    steps = list(range(outer))
    *before, first_turned = attention(0, turned, ())
    dq, dots, dq_lead, second_turned = attention(1, turned, before)
    carried = lax.ppermute(dq_lead, "seq", [(i, i + 1) for i in range(seq_size - 1)])
    first_send, first_kept = kv_part(0, turned, after(first_turned, dq), [steps])
    first_in = swapped(first_send, "seq", 1)
    odd_send, odd_kept, even_send, even_kept = kv_part(
        1, turned, after(second_turned, first_kept), [steps[1::2], steps[::2]]
    )
    own_dq, own_grads = call(
        functools.partial(own_kernel, offset),
        "own_tokens",
        [shape((row_count, cols + HD), BF16), shape((1, row_count, cols), BF16)],
        [dq, after(dots, odd_kept), carried],
        flops=OWN_FLOPS,
    )
    odd_in = swapped(after(odd_send, own_grads), "seq", 1)
    even_in = swapped(even_send, "seq", 1)
    dq_other = swapped(own_dq, "section", 1)

    def folded(kept, received, bit):
        while 2 * bit < outer:
            kept, send = fold(kept, received)
            received = swapped(send, "seq", 2 * bit)
            bit *= 2
        return kept, received

    first = folded(first_kept, first_in, 1)
    gathered = outer_gather(own_grads, outer, (first[0], *columns_mine[1:]))
    odd_sum = added(odd_kept, odd_in, BF16)
    second = folded(added(even_kept, even_in, F32), swapped(odd_sum, "seq", 2), 2)

    weight_keep, *weight_send = weight_part(columns_mine, columns_theirs, gathered)
    weight_in = three_ways(weight_send, 1)

    normed_keep, normed_dots, normed_send = normed_part(own_dq, dq_other, query_weight)
    normed_in = swapped(normed_send, "mp", 1)
    hidden_grad, norm_dot = call(
        functools.partial(hidden_kernel, model_width),
        "hidden_grad",
        [shape(hidden_part.shape, BF16), shape((1, row_count), F32)],
        [normed_keep, normed_in, normed_dots, hidden_part, gain_part, inv_rms],
    )

    kv_mine, *kv_send = outer_sums([*first, *second])
    kv_in = three_ways(kv_send, seq_size // 2)

    query_grad = call(
        query_grad_kernel,
        "query_grad",
        [shape((weight_keep.shape[0], local_cols), F32)],
        [weight_keep, *weight_in],
    )[0]
    kv_grad = call(
        kv_grad_kernel,
        "kv_grad",
        [shape((2, piece, local_cols), F32)],
        [after(kv_mine, query_grad), *kv_in],
    )[0]
    return (hidden_grad, query_grad, kv_grad, norm_dot.reshape(row_count))


def solution(mesh):
    placed = (
        P("seq", None),
        P(),
        P("seq", None, None),
        P(),
        P("section", "mp"),
        P(None, None, "mp"),
        P("seq", "mp"),
        P("seq", None),
        P("seq"),
    )
    return jax.shard_map(
        body,
        mesh=mesh,
        in_specs=placed,
        out_specs=(
            P("seq", ("section", "mp")),
            P(("section", "seq"), "mp"),
            P(None, ("section", "seq"), "mp"),
            P("seq"),
        ),
        check_vma=False,
    )
```

```python
import functools
import math

import jax
import jax.numpy as jnp
from jax import lax
from jax.experimental import pallas as pl
from jax.experimental.pallas import tpu as pltpu
from jax.sharding import PartitionSpec as P

HD = 128
EPSILON = 1e-06
MASKED = -1e30
LOG2_E = math.log2(math.e)
VMEM_BYTES = 24 * 1024 * 1024
CHUNKS = 2
NORM_FLOPS = 3_000_000_000
FIRST_ATTEND_FLOPS = 4_000_000_000
OUTER_FLOPS = 80_000_000
OWN_FLOPS = 2_000_000_000
ODD_FLOPS = 1_000_000_000

F32 = jnp.float32
BF16 = jnp.bfloat16

IN_VMEM = pl.BlockSpec(memory_space=pltpu.VMEM)
IN_SMEM = pl.BlockSpec(memory_space=pltpu.SMEM)
IN_HBM = pl.BlockSpec(memory_space=pltpu.HBM)


def shape(dims, kind):
    return jax.ShapeDtypeStruct(dims, kind)


def call(
    kernel, name, out_shape, operands, in_specs=None, scratch=(), flops=0, limit=VMEM_BYTES
):
    return pl.pallas_call(
        kernel,
        in_specs=in_specs or [IN_VMEM] * len(operands),
        out_specs=[IN_VMEM] * len(out_shape),
        out_shape=out_shape,
        scratch_shapes=scratch,
        compiler_params=pltpu.CompilerParams(vmem_limit_bytes=limit),
        cost_estimate=pl.CostEstimate(flops=flops, bytes_accessed=0, transcendentals=0),
        name=name,
    )(*operands)


def nt_dot(left, right):
    return lax.dot_general(left, right, (((1,), (1,)), ((), ())), preferred_element_type=F32)


def swapped(array, axis, mask):
    size = lax.axis_size(axis)
    return lax.ppermute(array, axis, [(i, i ^ mask) for i in range(size)])


def after(value, *others):
    return lax.optimization_barrier((value, *others))[0]


def lanes_at(ref, start, size):
    return ref[:, pl.ds(pl.multiple_of(start, size), size)]


def split_column(column):
    high = column.astype(BF16).astype(F32)
    rest = column - high
    middle = rest.astype(BF16).astype(F32)
    low = rest - middle
    lane = lax.broadcasted_iota(jnp.int32, (column.shape[0], HD), 1)
    terms = jnp.where(lane == 0, high, jnp.where(lane == 1, middle, jnp.where(lane == 2, low, 0.0)))
    return terms.astype(BF16)


def joined_column(terms):
    return jnp.sum(terms.astype(F32), axis=1, keepdims=True)


def norm_kernel(
    gain, hidden, hn, rms_out, hidden_part, gain_part, keep_out, send_out, gain_row, turned
):
    core = lax.axis_index("mp")
    width = hidden.shape[1]
    half = width // 2
    quarter = hidden_part.shape[1]
    gain_row[...] = gain[...].astype(F32).reshape(1, width)
    wide = hidden[...].astype(F32)
    inv_rms = lax.rsqrt(jnp.mean(wide * wide, axis=1, keepdims=True) + EPSILON)
    rms_out[...] = inv_rms
    hn[...] = (wide * inv_rms * gain_row[...]).astype(BF16)
    turned[...] = lanes_at(hn, core * half, half).T
    count, span = keep_out.shape[1:3]
    outer = lax.axis_index("seq") // 2
    for out, base in ((keep_out, 0), (send_out, count)):
        for step in range(count):
            start = pl.multiple_of((outer ^ (base + step)) * span, span)
            out[0, step] = turned[pl.ds(start, span), :]
    own = (2 * lax.axis_index("section") + core) * quarter
    hidden_part[...] = lanes_at(hidden, own, quarter)
    gain_part[...] = lanes_at(gain_row, own, quarter)


def norm_columns(hidden, gain, count):
    rows, width = hidden.shape
    half, quarter = width // 2, width // 4
    dims = (1, count // 2, half // count, rows)
    return call(
        norm_kernel,
        "norm_columns",
        [
            shape((rows, width), BF16),
            shape((rows, 1), F32),
            shape((rows, quarter), BF16),
            shape((1, quarter), F32),
            shape(dims, BF16),
            shape(dims, BF16),
        ],
        [gain, hidden],
        None,
        [pltpu.VMEM((1, width), F32), pltpu.VMEM((half, rows), BF16)],
        NORM_FLOPS,
    )


def query_kernel(hn, weight, grads, keep_out, send_out, pair_out, cross_out, total):
    section = lax.axis_index("section")
    half = weight.shape[0]
    lead = cross_out.shape[0]
    cols = keep_out.shape[1]
    total[...] = jnp.dot(
        lanes_at(hn, section * half, half), weight[...], preferred_element_type=F32
    )
    keep_out[...] = lanes_at(total, section * cols, cols)
    send_out[...] = lanes_at(total, (1 - section) * cols, cols).astype(BF16)
    pair_out[0] = keep_out[:lead].astype(BF16)
    pair_out[1] = grads[:lead, pl.ds(pl.multiple_of(section * cols, cols), cols)]
    cross_out[...] = send_out[:lead]


def query_part(hn, weight, attn_grad, lead):
    rows = hn.shape[0]
    local = weight.shape[1]
    cols = local // 2
    return call(
        query_kernel,
        "query_part",
        [
            shape((rows, cols), F32),
            shape((rows, cols), BF16),
            shape((2, lead, cols), BF16),
            shape((lead, cols), BF16),
        ],
        [hn, weight, attn_grad],
        None,
        [pltpu.VMEM((rows, local), F32)],
    )


def regroup_kernel(kept, received, keep_out, send_out):
    sources = kept.shape[0]
    count = keep_out.shape[1]
    for ref, place in ((kept, 0), (received, sources)):
        keep_out[place : place + sources] = ref[:, :count]
        send_out[place : place + sources] = ref[:, count:]


def columns_exchange(kept, received, count):
    bit = count // 2
    while bit > 1:
        sources, targets, *dims = kept.shape
        dims = (2 * sources, targets // 2, *dims)
        kept, send = call(
            regroup_kernel, "regroup", [shape(dims, BF16)] * 2, [kept, received]
        )
        bit //= 2
        received = swapped(send, "seq", 2 * bit)
    return kept, received


def pool_kernel(gain, states, weight, kv_out, turned_out):
    rows, width = states.shape
    cols = kv_out.shape[2]
    block = min(rows, 1024)
    start = pl.multiple_of(lax.axis_index("section") * cols, cols)
    gain_row = gain[...].astype(F32).reshape(1, width)
    for base in range(0, rows, block):
        part = slice(base, base + block)
        wide = states[part].astype(F32)
        inv_rms = lax.rsqrt(jnp.mean(wide * wide, axis=1, keepdims=True) + EPSILON)
        normed = (wide * inv_rms * gain_row).astype(BF16)
        for which in range(2):
            kv_out[which, part] = jnp.dot(
                normed, weight[which, :, pl.ds(start, cols)], preferred_element_type=F32
            ).astype(BF16)
        turned_out[:, part] = normed.T


def pool_project(states, gain, weight):
    rows, width = states.shape
    cols = weight.shape[2] // 2
    return call(
        pool_kernel,
        "pool_project",
        [shape((2, rows, cols), BF16), shape((width, rows), BF16)],
        [gain, states, weight],
    )


def rows_at(ref, start, size):
    if size % 8 == 0:
        return ref[pl.ds(pl.multiple_of(start, 8), size), :]
    window = (size + 14) // 8 * 8
    rest = start % 8
    wide = ref[pl.ds(pl.multiple_of(start - rest, 8), window), :]
    return pltpu.roll(wide, window - rest, 0)[:size]


def attend_kernel(
    chunk, slot_count, ids, counts, keep, other, pair, cross, grad_own, kv, *rest
):
    last = chunk == CHUNKS - 1
    if chunk > 0:
        before, dots_before, *rest = rest
    dq_out, dots_out, *rest = rest
    if last:
        lead_out, *rest = rest
    turned_kv, bias = rest
    section = lax.axis_index("section")
    rows, all_cols = keep.shape
    cols = all_cols // CHUNKS
    left = chunk * cols
    here = slice(left, left + cols)
    lead = cross.shape[0]
    keys = kv.shape[1]
    block_count = counts.shape[0]
    block_len = rows // block_count
    offset = block_len - 1
    length = keys // slot_count
    factor = 1.0 / math.sqrt(HD)
    slot_of = lax.broadcasted_iota(jnp.int32, (1, keys), 1) // length
    for block in range(block_count):
        line = jnp.full((1, keys), MASKED, F32)
        for slot in range(slot_count):
            opened = jnp.where(slot < counts[block], ids[block, slot], -1)
            line = jnp.where(slot_of == opened, 0.0, line)
        bias[block * block_len : (block + 1) * block_len, :] = jnp.broadcast_to(
            line, (block_len, keys)
        )
    following = lax.broadcasted_iota(jnp.int32, (rows, 1), 0) < offset
    own = keep[:, here] + other[:, here].astype(F32)
    led = pair[0, :, here].astype(F32) + cross[:, here].astype(F32)
    padding = jnp.zeros((rows - lead, cols), F32)
    queries = jnp.where(following, jnp.concatenate([led, padding], 0), own)
    own = lanes_at(grad_own, section * all_cols + left, cols).astype(F32)
    led = pair[1, :, here].astype(F32)
    grads = jnp.where(following, jnp.concatenate([led, padding], 0), own)
    rolled_queries = pltpu.roll(queries, rows - offset, 0)
    rolled_grads = pltpu.roll(grads, rows - offset, 0)
    dots = dots_before[...] if chunk > 0 else jnp.zeros((rows, 1), F32)
    if chunk > 0:
        dq_out[:, :left] = before[...]
    for head in range(cols // HD):
        span = slice(head * HD, (head + 1) * HD)
        at = slice(left + head * HD, left + (head + 1) * HD)
        query = rolled_queries[:, span].astype(BF16)
        grad = rolled_grads[:, span].astype(BF16)
        key = kv[0, :, at]
        value = kv[1, :, at]
        scores = nt_dot(query, key) * (factor * LOG2_E) + bias[...]
        peak = jnp.max(scores, axis=1, keepdims=True)
        weights = jnp.exp2(scores - peak)
        norm = 1.0 / jnp.sum(weights, axis=1, keepdims=True)
        grad_probs = nt_dot(grad, value)
        delta = jnp.sum(weights * grad_probs, axis=1, keepdims=True) * norm
        grad_scores = (weights * (grad_probs - delta)).astype(BF16)
        scale = norm * factor
        dq = jnp.dot(grad_scores, key, preferred_element_type=F32) * scale
        dq = pltpu.roll(dq, offset, 0).astype(BF16)
        dots = dots + jnp.sum(dq.astype(F32) * queries[:, span], axis=1, keepdims=True)
        dq_out[:, at] = dq
        turned_query = (query.astype(F32) * scale).T.astype(BF16)
        turned_grad = (rolled_grads[:, span] * norm).T.astype(BF16)
        turned_kv[span, :] = jnp.dot(
            turned_query, grad_scores, preferred_element_type=F32
        ).astype(BF16)
        turned_kv[cols + head * HD : cols + (head + 1) * HD, :] = jnp.dot(
            turned_grad, weights.astype(BF16), preferred_element_type=F32
        ).astype(BF16)
    if last:
        dots_out[...] = split_column(dots)
        lead_out[:, :all_cols] = dq_out[:lead]
        lead_out[:, all_cols:] = dots_out[:lead]
    else:
        dots_out[...] = dots


def kv_part_kernel(groups, turned, turned_kv, *rest):
    *outs, product = rest
    outer, inner_own = lax.axis_index("seq") // 2, lax.axis_index("seq") % 2
    width = turned.shape[0]
    product[:width] = nt_dot(turned[...], turned_kv[...])
    piece = outs[0].shape[2]
    half = width // 2
    for place, steps in enumerate(groups):
        for index, step in enumerate(steps):
            for part in range(2):
                for out, inner in ((outs[2 * place], 1 - inner_own), (outs[2 * place + 1], inner_own)):
                    start = part * half + (2 * (outer ^ step) + inner) * piece
                    out[index, part] = rows_at(product, start, piece).astype(out.dtype)


def attend(chunk, ids, counts, keep, other, pair, cross, attn_grad, kv, before):
    rows, all_cols = keep.shape
    cols = all_cols // CHUNKS
    lead = cross.shape[0]
    keys = kv.shape[1]
    last = chunk == CHUNKS - 1
    operands = [ids, counts, keep, other, pair, cross, attn_grad, kv, *before]
    out_shape = [
        shape((rows, (chunk + 1) * cols), BF16),
        shape((rows, HD), BF16) if last else shape((rows, 1), F32),
    ]
    if last:
        out_shape.append(shape((lead, all_cols + HD), BF16))
    out_shape.append(shape((2 * cols, keys), BF16))
    return call(
        functools.partial(attend_kernel, chunk, ids.shape[1]),
        "attend_%d" % chunk,
        out_shape,
        operands,
        [IN_SMEM] * 2 + [IN_VMEM] * (len(operands) - 2),
        [pltpu.VMEM((rows, keys), F32)],
        0 if last else FIRST_ATTEND_FLOPS,
    )


def kv_part(chunk, turned, turned_kv, groups):
    width = turned.shape[0]
    cols = turned_kv.shape[0]
    dims = (2, width // (2 * lax.axis_size("seq")), cols)
    return call(
        functools.partial(kv_part_kernel, groups),
        "kv_part_%d" % chunk,
        [shape((len(steps), *dims), kind) for steps in groups for kind in (BF16, F32)],
        [turned, turned_kv],
        None,
        [pltpu.VMEM((width + 16, cols), F32)],
    )


def own_kernel(offset, dq, dots, carried, out, grads_out):
    lead = carried.shape[0]
    cols = dq.shape[1]
    early = lax.broadcasted_iota(jnp.int32, (lead, 1), 0) < offset
    out[:lead, :cols] = jnp.where(early, carried[:, :cols], dq[:lead])
    out[:lead, cols:] = jnp.where(early, carried[:, cols:], dots[:lead])
    out[lead:, :cols] = dq[lead:]
    out[lead:, cols:] = dots[lead:]
    grads_out[0] = out[:, :cols]


def odd_kernel(first, first_in, second, second_in, out):
    for place in range(out.shape[1]):
        odd = 2 * place + 1
        out[0, place] = (first[odd] + first_in[odd].astype(F32)).astype(BF16)
        out[1, place] = (second[place] + second_in[place].astype(F32)).astype(BF16)


def even_kernel(first, first_in, second, second_in, out):
    for place in range(out.shape[1]):
        even = 2 * place
        out[0, place] = first[even] + first_in[even].astype(F32)
        out[1, place] = second[place] + second_in[place].astype(F32)


def both_chunks(kernel, name, kind, flops, *refs):
    dims = (CHUNKS, *refs[2].shape)
    return call(kernel, name, [shape(dims, kind)], list(refs), flops=flops)[0]


def fold_kernel(kept, received, keep_out, send_out):
    for place in range(keep_out.shape[1]):
        even, odd = 2 * place, 2 * place + 1
        keep_out[:, place] = kept[:, even] + received[:, even].astype(F32)
        send_out[:, place] = (kept[:, odd] + received[:, odd].astype(F32)).astype(BF16)


def fold(kept, received):
    chunks, count, *dims = kept.shape
    half = (chunks, count // 2, *dims)
    return call(fold_kernel, "fold", [shape(half, F32), shape(half, BF16)], [kept, received])


def outer_kernel(kept, received, mine, next_out, side_out, cross_out):
    section = lax.axis_index("section")
    for chunk in range(CHUNKS):
        for out, place, part in (
            (next_out, 1, section),
            (cross_out, 1, 1 - section),
            (side_out, 0, 1 - section),
            (mine, 0, section),
        ):
            total = kept[chunk, place, part] + received[chunk, place, part].astype(F32)
            out[chunk] = total.astype(out.dtype)


def outer_sums(kept, received):
    _, _, _, piece, cols = kept.shape
    dims = (CHUNKS, piece, cols)
    return call(
        outer_kernel, "outer_sums", [shape(dims, F32)] + [shape(dims, BF16)] * 3,
        [kept, received], flops=OUTER_FLOPS,
    )


def kv_grad_kernel(mine, following, side, cross, out):
    section = lax.axis_index("section")
    cols = mine.shape[2] // 2
    for chunk in range(CHUNKS):
        for which in range(2):
            span = slice(which * cols, (which + 1) * cols)
            own = mine[chunk, :, span] + following[chunk, :, span].astype(F32)
            other = side[chunk, :, span].astype(F32) + cross[chunk, :, span].astype(F32)
            for value, part in ((own, section), (other, 1 - section)):
                start = pl.multiple_of((part * CHUNKS + chunk) * cols, cols)
                out[which, :, pl.ds(start, cols)] = value


def weight_kernel(*refs):
    *refs, keep_out, pair_out, side_out, cross_out = refs
    mine, theirs, grads = refs[:2], refs[2:4], refs[4:]
    section = lax.axis_index("section")
    inner_own = lax.axis_index("seq") % 2
    swap = lax.axis_index("mp") != section
    piece = keep_out.shape[0]
    gathered = [ref[index] for ref in grads for index in range(ref.shape[0])]
    half = len(gathered) // 2
    for outs, inner, other in (
        (pair_out, 1 - inner_own, False),
        (cross_out, 1 - inner_own, True),
        (side_out, inner_own, True),
        (keep_out, inner_own, False),
    ):
        rows = pl.ds(pl.multiple_of(inner * piece, piece), piece)
        total = None
        for place, grad in enumerate(gathered):
            same, opposite = (refs[place // half][place % half, 0, rows, :] for refs in (mine, theirs))
            if other:
                same, opposite = opposite, same
            column = jnp.where(swap, opposite, same)
            term = jnp.dot(column, grad, preferred_element_type=F32)
            total = term if total is None else total + term
        outs[...] = total.astype(outs.dtype)


def weight_part(mine, theirs, grads):
    dims = (mine[0].shape[2] // 2, grads[0].shape[2])
    return call(
        weight_kernel,
        "weight_part",
        [shape(dims, F32)] + [shape(dims, BF16)] * 3,
        [*mine, *theirs, *grads],
    )


def stack_kernel(*refs):
    *refs, out = refs
    start = 0
    for ref in refs:
        out[start : start + ref.shape[0]] = ref[...]
        start += ref.shape[0]


def outer_gather(piece, count, ahead):
    stages, whole = [piece], piece
    bit = count // 2
    while bit:
        if len(stages) > 1:
            whole = call(
                stack_kernel,
                "stacked",
                [shape((2 * whole.shape[0], *piece.shape[1:]), BF16)],
                [after(stages[0], *ahead), *stages[1:]],
            )[0]
        stages.append(swapped(whole, "seq", 2 * bit))
        bit //= 2
    return stages


def query_grad_kernel(kept, paired, side, cross, out):
    section = lax.axis_index("section")
    cols = kept.shape[1]
    own = pl.ds(pl.multiple_of(section * cols, cols), cols)
    out[:, own] = kept[...] + paired[...].astype(F32)
    other = pl.ds(pl.multiple_of((1 - section) * cols, cols), cols)
    out[:, other] = side[...].astype(F32) + cross[...].astype(F32)


def normed_kernel(own, other, weight, keep_out, dots_out, send_out, total):
    cols = own.shape[1] - HD
    swap = lax.axis_index("section") == 1
    core = lax.axis_index("mp")
    quarter = keep_out.shape[1]
    first = jnp.where(swap, other[:, :cols], own[:, :cols])
    second = jnp.where(swap, own[:, :cols], other[:, :cols])
    total[...] = nt_dot(first, weight[:, :cols]) + nt_dot(second, weight[:, cols:])
    keep_out[...] = lanes_at(total, core * quarter, quarter)
    send_out[:, :quarter] = lanes_at(total, (1 - core) * quarter, quarter).astype(BF16)
    dots = joined_column(own[:, cols:]) + joined_column(other[:, cols:])
    dots_out[...] = dots
    send_out[:, quarter:] = split_column(dots)


def normed_part(own, other, weight):
    rows = own.shape[0]
    half = weight.shape[0]
    quarter = half // 2
    return call(
        normed_kernel,
        "normed_part",
        [shape((rows, quarter), F32), shape((rows, 1), F32), shape((rows, quarter + HD), BF16)],
        [own, other, weight],
        None,
        [pltpu.VMEM((rows, half), F32)],
    )


def hidden_kernel(width, kept, received, dots, hidden, gain, inv_rms, grad_out, dot_out):
    quarter = kept.shape[1]
    inv = inv_rms[...]
    row_dot = (dots[...] + joined_column(received[:, quarter:])) / inv
    wide = jnp.broadcast_to(row_dot * (1.0 / math.sqrt(width)), (row_dot.shape[0], HD))
    dot_out[...] = wide.T[:1]
    scaled = gain[...] * (kept[...] + received[:, :quarter].astype(F32))
    grad_out[...] = (
        inv * scaled - hidden[...].astype(F32) * (inv * inv * inv * row_dot * (1.0 / width))
    ).astype(BF16)


def body(
    hidden,
    hidden_gain,
    neighbour_states,
    encoder_gain,
    query_weight,
    kv_weight,
    attn_grad,
    neighbour_ids,
    valid_counts,
):
    seq_size = lax.axis_size("seq")
    outer = seq_size // 2
    row_count, model_width = hidden.shape
    local_cols = query_weight.shape[1]
    cols = local_cols // 2
    slot_total, nb_length, enc_width = neighbour_states.shape
    block_len = row_count // neighbour_ids.shape[0]
    offset = block_len - 1
    piece = enc_width // (2 * seq_size)
    backward = [(i, i - 1) for i in range(1, seq_size)]

    hn, inv_rms, hidden_part, gain_part, columns_kept, columns_send = norm_columns(
        hidden, hidden_gain, outer
    )
    keep, send, pair, cross = query_part(hn, query_weight, attn_grad, block_len)
    other = swapped(send, "section", 1)
    pair_in = lax.ppermute(pair, "seq", backward)
    cross_in = lax.ppermute(
        cross,
        ("section", "seq"),
        [(s * seq_size + i, (1 - s) * seq_size + j) for s in range(2) for i, j in backward],
    )
    kv, turned = pool_project(
        neighbour_states.reshape(slot_total * nb_length, enc_width), encoder_gain, kv_weight
    )

    def attention(chunk, ahead, before):
        return attend(
            chunk, neighbour_ids, valid_counts, after(keep, ahead), other, pair_in, cross_in,
            attn_grad, kv, before,
        )

    def three_ways(pieces, mask):
        near, side, cross = pieces
        pairs = [(s * seq_size + i, (1 - s) * seq_size + (i ^ mask)) for s in range(2) for i in range(seq_size)]
        crossed = lax.ppermute(cross, ("section", "seq"), pairs)
        return swapped(near, "seq", mask), swapped(side, "section", 1), crossed

    columns_in = swapped(columns_send, "seq", outer)
    columns_mine = columns_exchange(columns_kept, columns_in, outer)
    columns_theirs = [swapped(column, "mp", 1) for column in columns_mine]

    steps = list(range(outer))
    *before, first_turned = attention(0, turned, ())
    dq, dots, dq_lead, second_turned = attention(1, turned, before)
    carried = lax.ppermute(dq_lead, "seq", [(i, i + 1) for i in range(seq_size - 1)])
    first_send, first_kept = kv_part(0, turned, after(first_turned, dq), [steps])
    first_in = swapped(first_send, "seq", 1)
    odd_send, odd_kept, even_send, even_kept = kv_part(
        1, turned, after(second_turned, first_kept), [steps[1::2], steps[::2]]
    )
    own_dq, own_grads = call(
        functools.partial(own_kernel, offset),
        "own_tokens",
        [shape((row_count, cols + HD), BF16), shape((1, row_count, cols), BF16)],
        [dq, dots, carried],
        flops=OWN_FLOPS,
    )
    odd_in = swapped(after(odd_send, own_grads), "seq", 1)
    even_in = swapped(even_send, "seq", 1)
    dq_other = swapped(own_dq, "section", 1)

    gathered = outer_gather(own_grads, outer, columns_mine[1:])

    odd_sums = both_chunks(
        odd_kernel, "odd_sums", BF16, ODD_FLOPS, first_kept, first_in, odd_kept, odd_in
    )
    kv_received = swapped(odd_sums, "seq", 2)
    kv_kept = both_chunks(
        even_kernel, "even_sums", F32, 0, first_kept, first_in, even_kept, even_in
    )
    bit = 2
    while 2 * bit < outer:
        kv_kept, kv_send = fold(kv_kept, kv_received)
        kv_received = swapped(kv_send, "seq", 2 * bit)
        bit *= 2

    weight_keep, *weight_send = weight_part(columns_mine, columns_theirs, gathered)
    weight_in = three_ways(weight_send, 1)

    normed_keep, normed_dots, normed_send = normed_part(own_dq, dq_other, query_weight)
    normed_in = swapped(normed_send, "mp", 1)
    hidden_grad, norm_dot = call(
        functools.partial(hidden_kernel, model_width),
        "hidden_grad",
        [shape(hidden_part.shape, BF16), shape((1, row_count), F32)],
        [normed_keep, normed_in, normed_dots, hidden_part, gain_part, inv_rms],
    )

    kv_mine, *kv_send = outer_sums(kv_kept, kv_received)
    kv_in = three_ways(kv_send, seq_size // 2)

    query_grad = call(
        query_grad_kernel,
        "query_grad",
        [shape((weight_keep.shape[0], local_cols), F32)],
        [weight_keep, *weight_in],
    )[0]
    kv_grad = call(
        kv_grad_kernel,
        "kv_grad",
        [shape((2, piece, local_cols), F32)],
        [after(kv_mine, query_grad), *kv_in],
    )[0]
    return (hidden_grad, query_grad, kv_grad, norm_dot.reshape(row_count))


def solution(mesh):
    placed = (
        P("seq", None),
        P(),
        P("seq", None, None),
        P(),
        P("section", "mp"),
        P(None, None, "mp"),
        P("seq", "mp"),
        P("seq", None),
        P("seq"),
    )
    return jax.shard_map(
        body,
        mesh=mesh,
        in_specs=placed,
        out_specs=(
            P("seq", ("section", "mp")),
            P(("section", "seq"), "mp"),
            P(None, ("section", "seq"), "mp"),
            P("seq"),
        ),
        check_vma=False,
    )
```

```python
import functools
import math

import jax
import jax.numpy as jnp
from jax import lax
from jax.experimental import pallas as pl
from jax.experimental.pallas import tpu as pltpu
from jax.sharding import PartitionSpec as P

HD = 128
EPSILON = 1e-06
MASKED = -1e30
LOG2_E = math.log2(math.e)
VMEM_BYTES = 24 * 1024 * 1024
CHUNKS = 2
NORM_FLOPS = 3_000_000_000
ATTEND_FLOPS = 4_000_000_000
OUTER_FLOPS = 80_000_000
OWN_FLOPS = 2_000_000_000
ODD_FLOPS = 1_000_000_000

F32 = jnp.float32
BF16 = jnp.bfloat16

IN_VMEM = pl.BlockSpec(memory_space=pltpu.VMEM)
IN_SMEM = pl.BlockSpec(memory_space=pltpu.SMEM)
IN_HBM = pl.BlockSpec(memory_space=pltpu.HBM)


def shape(dims, kind):
    return jax.ShapeDtypeStruct(dims, kind)


def call(
    kernel, name, out_shape, operands, in_specs=None, scratch=(), flops=0, limit=VMEM_BYTES
):
    return pl.pallas_call(
        kernel,
        in_specs=in_specs or [IN_VMEM] * len(operands),
        out_specs=[IN_VMEM] * len(out_shape),
        out_shape=out_shape,
        scratch_shapes=scratch,
        compiler_params=pltpu.CompilerParams(vmem_limit_bytes=limit),
        cost_estimate=pl.CostEstimate(flops=flops, bytes_accessed=0, transcendentals=0),
        name=name,
    )(*operands)


def nt_dot(left, right):
    return lax.dot_general(left, right, (((1,), (1,)), ((), ())), preferred_element_type=F32)


def swapped(array, axis, mask):
    size = lax.axis_size(axis)
    return lax.ppermute(array, axis, [(i, i ^ mask) for i in range(size)])


def after(value, *others):
    return lax.optimization_barrier((value, *others))[0]


def lanes_at(ref, start, size):
    return ref[:, pl.ds(pl.multiple_of(start, size), size)]


def split_column(column):
    high = column.astype(BF16).astype(F32)
    rest = column - high
    middle = rest.astype(BF16).astype(F32)
    low = rest - middle
    lane = lax.broadcasted_iota(jnp.int32, (column.shape[0], HD), 1)
    terms = jnp.where(lane == 0, high, jnp.where(lane == 1, middle, jnp.where(lane == 2, low, 0.0)))
    return terms.astype(BF16)


def joined_column(terms):
    return jnp.sum(terms.astype(F32), axis=1, keepdims=True)


def norm_kernel(
    gain, hidden, hn, rms_out, hidden_part, gain_part, keep_out, send_out, gain_row, turned
):
    core = lax.axis_index("mp")
    width = hidden.shape[1]
    half = width // 2
    quarter = hidden_part.shape[1]
    gain_row[...] = gain[...].astype(F32).reshape(1, width)
    wide = hidden[...].astype(F32)
    inv_rms = lax.rsqrt(jnp.mean(wide * wide, axis=1, keepdims=True) + EPSILON)
    rms_out[...] = inv_rms
    hn[...] = (wide * inv_rms * gain_row[...]).astype(BF16)
    turned[...] = lanes_at(hn, core * half, half).T
    count, span = keep_out.shape[1:3]
    outer = lax.axis_index("seq") // 2
    for out, base in ((keep_out, 0), (send_out, count)):
        for step in range(count):
            start = pl.multiple_of((outer ^ (base + step)) * span, span)
            out[0, step] = turned[pl.ds(start, span), :]
    own = (2 * lax.axis_index("section") + core) * quarter
    hidden_part[...] = lanes_at(hidden, own, quarter)
    gain_part[...] = lanes_at(gain_row, own, quarter)


def norm_columns(hidden, gain, count):
    rows, width = hidden.shape
    half, quarter = width // 2, width // 4
    dims = (1, count // 2, half // count, rows)
    return call(
        norm_kernel,
        "norm_columns",
        [
            shape((rows, width), BF16),
            shape((rows, 1), F32),
            shape((rows, quarter), BF16),
            shape((1, quarter), F32),
            shape(dims, BF16),
            shape(dims, BF16),
        ],
        [gain, hidden],
        None,
        [pltpu.VMEM((1, width), F32), pltpu.VMEM((half, rows), BF16)],
        NORM_FLOPS,
    )


def query_kernel(hn, weight, grads, keep_out, send_out, pair_out, cross_out, total):
    section = lax.axis_index("section")
    half = weight.shape[0]
    lead = cross_out.shape[0]
    cols = keep_out.shape[1]
    total[...] = jnp.dot(
        lanes_at(hn, section * half, half), weight[...], preferred_element_type=F32
    )
    keep_out[...] = lanes_at(total, section * cols, cols)
    send_out[...] = lanes_at(total, (1 - section) * cols, cols).astype(BF16)
    pair_out[0] = keep_out[:lead].astype(BF16)
    pair_out[1] = grads[:lead, pl.ds(pl.multiple_of(section * cols, cols), cols)]
    cross_out[...] = send_out[:lead]


def query_part(hn, weight, attn_grad, lead):
    rows = hn.shape[0]
    local = weight.shape[1]
    cols = local // 2
    return call(
        query_kernel,
        "query_part",
        [
            shape((rows, cols), F32),
            shape((rows, cols), BF16),
            shape((2, lead, cols), BF16),
            shape((lead, cols), BF16),
        ],
        [hn, weight, attn_grad],
        None,
        [pltpu.VMEM((rows, local), F32)],
    )


def regroup_kernel(kept, received, keep_out, send_out):
    sources = kept.shape[0]
    count = keep_out.shape[1]
    for ref, place in ((kept, 0), (received, sources)):
        keep_out[place : place + sources] = ref[:, :count]
        send_out[place : place + sources] = ref[:, count:]


def columns_exchange(kept, received, count):
    bit = count // 2
    while bit > 1:
        sources, targets, *dims = kept.shape
        dims = (2 * sources, targets // 2, *dims)
        kept, send = call(
            regroup_kernel, "regroup", [shape(dims, BF16)] * 2, [kept, received]
        )
        bit //= 2
        received = swapped(send, "seq", 2 * bit)
    return kept, received


def pool_kernel(gain, states, weight, kv_out, turned_out):
    rows, width = states.shape
    cols = kv_out.shape[2]
    block = min(rows, 1024)
    start = pl.multiple_of(lax.axis_index("section") * cols, cols)
    gain_row = gain[...].astype(F32).reshape(1, width)
    for base in range(0, rows, block):
        part = slice(base, base + block)
        wide = states[part].astype(F32)
        inv_rms = lax.rsqrt(jnp.mean(wide * wide, axis=1, keepdims=True) + EPSILON)
        normed = (wide * inv_rms * gain_row).astype(BF16)
        for which in range(2):
            kv_out[which, part] = jnp.dot(
                normed, weight[which, :, pl.ds(start, cols)], preferred_element_type=F32
            ).astype(BF16)
        turned_out[:, part] = normed.T


def pool_project(states, gain, weight):
    rows, width = states.shape
    cols = weight.shape[2] // 2
    return call(
        pool_kernel,
        "pool_project",
        [shape((2, rows, cols), BF16), shape((width, rows), BF16)],
        [gain, states, weight],
    )


def rows_at(ref, start, size):
    if size % 8 == 0:
        return ref[pl.ds(pl.multiple_of(start, 8), size), :]
    window = (size + 14) // 8 * 8
    rest = start % 8
    wide = ref[pl.ds(pl.multiple_of(start - rest, 8), window), :]
    return pltpu.roll(wide, window - rest, 0)[:size]


def attend_kernel(
    slot_count, ids, counts, keep, other, pair, cross, grad_own, kv, dq_out, dots_out, lead_out, *rest
):
    *turned_kv, bias = rest
    section = lax.axis_index("section")
    rows, cols = keep.shape
    lead = cross.shape[0]
    keys = kv.shape[1]
    block_count = counts.shape[0]
    block_len = rows // block_count
    offset = block_len - 1
    length = keys // slot_count
    factor = 1.0 / math.sqrt(HD)
    slot_of = lax.broadcasted_iota(jnp.int32, (1, keys), 1) // length
    for block in range(block_count):
        line = jnp.full((1, keys), MASKED, F32)
        for slot in range(slot_count):
            opened = jnp.where(slot < counts[block], ids[block, slot], -1)
            line = jnp.where(slot_of == opened, 0.0, line)
        bias[block * block_len : (block + 1) * block_len, :] = jnp.broadcast_to(
            line, (block_len, keys)
        )
    following = lax.broadcasted_iota(jnp.int32, (rows, 1), 0) < offset
    own = keep[...] + other[...].astype(F32)
    led = pair[0].astype(F32) + cross[...].astype(F32)
    padding = jnp.zeros((rows - lead, cols), F32)
    queries = jnp.where(following, jnp.concatenate([led, padding], 0), own)
    own = lanes_at(grad_own, section * cols, cols).astype(F32)
    grads = jnp.where(following, jnp.concatenate([pair[1].astype(F32), padding], 0), own)
    rolled_queries = pltpu.roll(queries, rows - offset, 0)
    rolled_grads = pltpu.roll(grads, rows - offset, 0)
    dots = jnp.zeros((rows, 1), F32)
    span = cols // CHUNKS
    for head in range(cols // HD):
        at = slice(head * HD, (head + 1) * HD)
        query = rolled_queries[:, at].astype(BF16)
        grad = rolled_grads[:, at].astype(BF16)
        key = kv[0, :, at]
        value = kv[1, :, at]
        scores = nt_dot(query, key) * (factor * LOG2_E) + bias[...]
        peak = jnp.max(scores, axis=1, keepdims=True)
        weights = jnp.exp2(scores - peak)
        norm = 1.0 / jnp.sum(weights, axis=1, keepdims=True)
        grad_probs = nt_dot(grad, value)
        delta = jnp.sum(weights * grad_probs, axis=1, keepdims=True) * norm
        grad_scores = (weights * (grad_probs - delta)).astype(BF16)
        scale = norm * factor
        dq = jnp.dot(grad_scores, key, preferred_element_type=F32) * scale
        dq = pltpu.roll(dq, offset, 0).astype(BF16)
        dots = dots + jnp.sum(dq.astype(F32) * queries[:, at], axis=1, keepdims=True)
        dq_out[:, at] = dq
        turned_query = (query.astype(F32) * scale).T.astype(BF16)
        turned_grad = (rolled_grads[:, at] * norm).T.astype(BF16)
        out = turned_kv[head * HD // span]
        base = head * HD % span
        out[base : base + HD, :] = jnp.dot(
            turned_query, grad_scores, preferred_element_type=F32
        ).astype(BF16)
        out[span + base : span + base + HD, :] = jnp.dot(
            turned_grad, weights.astype(BF16), preferred_element_type=F32
        ).astype(BF16)
    dots_out[...] = split_column(dots)
    lead_out[:, :cols] = dq_out[:lead]
    lead_out[:, cols:] = dots_out[:lead]


def kv_part_kernel(groups, turned, turned_kv, *rest):
    *outs, product = rest
    outer, inner_own = lax.axis_index("seq") // 2, lax.axis_index("seq") % 2
    width = turned.shape[0]
    product[:width] = nt_dot(turned[...], turned_kv[...])
    piece = outs[0].shape[2]
    half = width // 2
    for place, steps in enumerate(groups):
        for index, step in enumerate(steps):
            for part in range(2):
                for out, inner in ((outs[2 * place], 1 - inner_own), (outs[2 * place + 1], inner_own)):
                    start = part * half + (2 * (outer ^ step) + inner) * piece
                    out[index, part] = rows_at(product, start, piece).astype(out.dtype)


def attend(ids, counts, keep, other, pair, cross, attn_grad, kv):
    rows, cols = keep.shape
    lead = cross.shape[0]
    keys = kv.shape[1]
    operands = [ids, counts, keep, other, pair, cross, attn_grad, kv]
    return call(
        functools.partial(attend_kernel, ids.shape[1]),
        "attend",
        [
            shape((rows, cols), BF16),
            shape((rows, HD), BF16),
            shape((lead, cols + HD), BF16),
            *[shape((2 * cols // CHUNKS, keys), BF16)] * CHUNKS,
        ],
        operands,
        [IN_SMEM] * 2 + [IN_VMEM] * (len(operands) - 2),
        [pltpu.VMEM((rows, keys), F32)],
        ATTEND_FLOPS,
    )


def kv_part(chunk, turned, turned_kv, groups):
    width = turned.shape[0]
    cols = turned_kv.shape[0]
    dims = (2, width // (2 * lax.axis_size("seq")), cols)
    return call(
        functools.partial(kv_part_kernel, groups),
        "kv_part_%d" % chunk,
        [shape((len(steps), *dims), kind) for steps in groups for kind in (BF16, F32)],
        [turned, turned_kv],
        None,
        [pltpu.VMEM((width + 16, cols), F32)],
    )


def own_kernel(offset, dq, dots, carried, out, grads_out):
    lead = carried.shape[0]
    cols = dq.shape[1]
    early = lax.broadcasted_iota(jnp.int32, (lead, 1), 0) < offset
    out[:lead, :cols] = jnp.where(early, carried[:, :cols], dq[:lead])
    out[:lead, cols:] = jnp.where(early, carried[:, cols:], dots[:lead])
    out[lead:, :cols] = dq[lead:]
    out[lead:, cols:] = dots[lead:]
    grads_out[0] = out[:, :cols]


def odd_kernel(first, first_in, second, second_in, out):
    for place in range(out.shape[1]):
        odd = 2 * place + 1
        out[0, place] = (first[odd] + first_in[odd].astype(F32)).astype(BF16)
        out[1, place] = (second[place] + second_in[place].astype(F32)).astype(BF16)


def even_kernel(first, first_in, second, second_in, out):
    for place in range(out.shape[1]):
        even = 2 * place
        out[0, place] = first[even] + first_in[even].astype(F32)
        out[1, place] = second[place] + second_in[place].astype(F32)


def both_chunks(kernel, name, kind, flops, *refs):
    dims = (CHUNKS, *refs[2].shape)
    return call(kernel, name, [shape(dims, kind)], list(refs), flops=flops)[0]


def fold_kernel(kept, received, keep_out, send_out):
    for place in range(keep_out.shape[1]):
        even, odd = 2 * place, 2 * place + 1
        keep_out[:, place] = kept[:, even] + received[:, even].astype(F32)
        send_out[:, place] = (kept[:, odd] + received[:, odd].astype(F32)).astype(BF16)


def fold(kept, received):
    chunks, count, *dims = kept.shape
    half = (chunks, count // 2, *dims)
    return call(fold_kernel, "fold", [shape(half, F32), shape(half, BF16)], [kept, received])


def outer_kernel(kept, received, mine, next_out, side_out, cross_out):
    section = lax.axis_index("section")
    for chunk in range(CHUNKS):
        for out, place, part in (
            (next_out, 1, section),
            (cross_out, 1, 1 - section),
            (side_out, 0, 1 - section),
            (mine, 0, section),
        ):
            total = kept[chunk, place, part] + received[chunk, place, part].astype(F32)
            out[chunk] = total.astype(out.dtype)


def outer_sums(kept, received):
    _, _, _, piece, cols = kept.shape
    dims = (CHUNKS, piece, cols)
    return call(
        outer_kernel, "outer_sums", [shape(dims, F32)] + [shape(dims, BF16)] * 3,
        [kept, received], flops=OUTER_FLOPS,
    )


def kv_grad_kernel(mine, following, cross, side, out):
    section = lax.axis_index("section")
    cols = mine.shape[2] // 2
    for chunk in range(CHUNKS):
        for which in range(2):
            span = slice(which * cols, (which + 1) * cols)
            own = mine[chunk, :, span] + following[chunk, :, span].astype(F32)
            other = side[chunk, :, span].astype(F32) + cross[chunk, :, span].astype(F32)
            for value, part in ((own, section), (other, 1 - section)):
                start = pl.multiple_of((part * CHUNKS + chunk) * cols, cols)
                out[which, :, pl.ds(start, cols)] = value


def weight_kernel(*refs):
    *refs, keep_out, pair_out, side_out, cross_out = refs
    mine, theirs, grads = refs[:2], refs[2:4], refs[4:]
    section = lax.axis_index("section")
    inner_own = lax.axis_index("seq") % 2
    swap = lax.axis_index("mp") != section
    piece = keep_out.shape[0]
    gathered = [ref[index] for ref in grads for index in range(ref.shape[0])]
    half = len(gathered) // 2
    for outs, inner, other in (
        (pair_out, 1 - inner_own, False),
        (cross_out, 1 - inner_own, True),
        (side_out, inner_own, True),
        (keep_out, inner_own, False),
    ):
        rows = pl.ds(pl.multiple_of(inner * piece, piece), piece)
        total = None
        for place, grad in enumerate(gathered):
            same, opposite = (refs[place // half][place % half, 0, rows, :] for refs in (mine, theirs))
            if other:
                same, opposite = opposite, same
            column = jnp.where(swap, opposite, same)
            term = jnp.dot(column, grad, preferred_element_type=F32)
            total = term if total is None else total + term
        outs[...] = total.astype(outs.dtype)


def weight_part(mine, theirs, grads):
    dims = (mine[0].shape[2] // 2, grads[0].shape[2])
    return call(
        weight_kernel,
        "weight_part",
        [shape(dims, F32)] + [shape(dims, BF16)] * 3,
        [*mine, *theirs, *grads],
    )


def stack_kernel(*refs):
    *refs, out = refs
    start = 0
    for ref in refs:
        out[start : start + ref.shape[0]] = ref[...]
        start += ref.shape[0]


def outer_gather(piece, count, ahead):
    stages, whole = [piece], piece
    bit = count // 2
    while bit:
        if len(stages) > 1:
            whole = call(
                stack_kernel,
                "stacked",
                [shape((2 * whole.shape[0], *piece.shape[1:]), BF16)],
                [after(stages[0], *ahead), *stages[1:]],
            )[0]
        stages.append(swapped(whole, "seq", 2 * bit))
        bit //= 2
    return stages


def query_grad_kernel(kept, paired, cross, side, out):
    section = lax.axis_index("section")
    cols = kept.shape[1]
    own = pl.ds(pl.multiple_of(section * cols, cols), cols)
    out[:, own] = kept[...] + paired[...].astype(F32)
    other = pl.ds(pl.multiple_of((1 - section) * cols, cols), cols)
    out[:, other] = side[...].astype(F32) + cross[...].astype(F32)


def normed_kernel(own, other, weight, keep_out, dots_out, send_out, total):
    cols = own.shape[1] - HD
    swap = lax.axis_index("section") == 1
    core = lax.axis_index("mp")
    quarter = keep_out.shape[1]
    first = jnp.where(swap, other[:, :cols], own[:, :cols])
    second = jnp.where(swap, own[:, :cols], other[:, :cols])
    total[...] = nt_dot(first, weight[:, :cols]) + nt_dot(second, weight[:, cols:])
    keep_out[...] = lanes_at(total, core * quarter, quarter)
    send_out[:, :quarter] = lanes_at(total, (1 - core) * quarter, quarter).astype(BF16)
    dots = joined_column(own[:, cols:]) + joined_column(other[:, cols:])
    dots_out[...] = dots
    send_out[:, quarter:] = split_column(dots)


def normed_part(own, other, weight):
    rows = own.shape[0]
    half = weight.shape[0]
    quarter = half // 2
    return call(
        normed_kernel,
        "normed_part",
        [shape((rows, quarter), F32), shape((rows, 1), F32), shape((rows, quarter + HD), BF16)],
        [own, other, weight],
        None,
        [pltpu.VMEM((rows, half), F32)],
    )


def hidden_kernel(width, kept, received, dots, hidden, gain, inv_rms, grad_out, dot_out):
    quarter = kept.shape[1]
    inv = inv_rms[...]
    row_dot = (dots[...] + joined_column(received[:, quarter:])) / inv
    wide = jnp.broadcast_to(row_dot * (1.0 / math.sqrt(width)), (row_dot.shape[0], HD))
    dot_out[...] = wide.T[:1]
    scaled = gain[...] * (kept[...] + received[:, :quarter].astype(F32))
    grad_out[...] = (
        inv * scaled - hidden[...].astype(F32) * (inv * inv * inv * row_dot * (1.0 / width))
    ).astype(BF16)


def body(
    hidden,
    hidden_gain,
    neighbour_states,
    encoder_gain,
    query_weight,
    kv_weight,
    attn_grad,
    neighbour_ids,
    valid_counts,
):
    seq_size = lax.axis_size("seq")
    outer = seq_size // 2
    row_count, model_width = hidden.shape
    local_cols = query_weight.shape[1]
    cols = local_cols // 2
    slot_total, nb_length, enc_width = neighbour_states.shape
    block_len = row_count // neighbour_ids.shape[0]
    offset = block_len - 1
    piece = enc_width // (2 * seq_size)
    backward = [(i, i - 1) for i in range(1, seq_size)]

    hn, inv_rms, hidden_part, gain_part, columns_kept, columns_send = norm_columns(
        hidden, hidden_gain, outer
    )
    keep, send, pair, cross = query_part(hn, query_weight, attn_grad, block_len)
    other = swapped(send, "section", 1)
    pair_in = lax.ppermute(pair, "seq", backward)
    cross_in = lax.ppermute(
        cross,
        ("section", "seq"),
        [(s * seq_size + i, (1 - s) * seq_size + j) for s in range(2) for i, j in backward],
    )
    kv, turned = pool_project(
        neighbour_states.reshape(slot_total * nb_length, enc_width), encoder_gain, kv_weight
    )

    def three_ways(pieces, mask):
        near, side, cross = pieces
        pairs = [(s * seq_size + i, (1 - s) * seq_size + (i ^ mask)) for s in range(2) for i in range(seq_size)]
        return (
            swapped(near, "seq", mask),
            lax.ppermute(cross, ("section", "seq"), pairs),
            swapped(side, "section", 1),
        )

    columns_in = swapped(columns_send, "seq", outer)
    columns_mine = columns_exchange(columns_kept, columns_in, outer)
    columns_theirs = [swapped(column, "mp", 1) for column in columns_mine]

    steps = list(range(outer))
    dq, dots, dq_lead, first_turned, second_turned = attend(
        neighbour_ids, valid_counts, after(keep, turned), other, pair_in, cross_in, attn_grad, kv
    )
    carried = lax.ppermute(dq_lead, "seq", [(i, i + 1) for i in range(seq_size - 1)])
    first_send, first_kept = kv_part(0, turned, after(first_turned, dq), [steps])
    first_in = swapped(first_send, "seq", 1)
    own_dq, own_grads = call(
        functools.partial(own_kernel, offset),
        "own_tokens",
        [shape((row_count, cols + HD), BF16), shape((1, row_count, cols), BF16)],
        [dq, dots, carried],
        flops=OWN_FLOPS,
    )
    odd_send, odd_kept, even_send, even_kept = kv_part(
        1, turned, after(second_turned, first_kept), [steps[1::2], steps[::2]]
    )
    odd_in = swapped(after(odd_send, own_grads), "seq", 1)
    even_in = swapped(even_send, "seq", 1)
    dq_other = swapped(own_dq, "section", 1)

    gathered = outer_gather(own_grads, outer, columns_mine[1:])

    odd_sums = both_chunks(
        odd_kernel, "odd_sums", BF16, ODD_FLOPS, first_kept, first_in, odd_kept, odd_in
    )
    kv_received = swapped(odd_sums, "seq", 2)
    kv_kept = both_chunks(
        even_kernel, "even_sums", F32, 0, first_kept, first_in, even_kept, even_in
    )
    bit = 2
    while 2 * bit < outer:
        kv_kept, kv_send = fold(kv_kept, kv_received)
        kv_received = swapped(kv_send, "seq", 2 * bit)
        bit *= 2

    weight_keep, *weight_send = weight_part(columns_mine, columns_theirs, gathered)
    weight_in = three_ways(weight_send, 1)

    normed_keep, normed_dots, normed_send = normed_part(own_dq, dq_other, query_weight)
    normed_in = swapped(normed_send, "mp", 1)
    hidden_grad, norm_dot = call(
        functools.partial(hidden_kernel, model_width),
        "hidden_grad",
        [shape(hidden_part.shape, BF16), shape((1, row_count), F32)],
        [normed_keep, normed_in, normed_dots, hidden_part, gain_part, inv_rms],
    )

    kv_mine, *kv_send = outer_sums(kv_kept, kv_received)
    kv_in = three_ways(kv_send, seq_size // 2)

    query_grad = call(
        query_grad_kernel,
        "query_grad",
        [shape((weight_keep.shape[0], local_cols), F32)],
        [weight_keep, *weight_in],
    )[0]
    kv_grad = call(
        kv_grad_kernel,
        "kv_grad",
        [shape((2, piece, local_cols), F32)],
        [after(kv_mine, query_grad), *kv_in],
    )[0]
    return (hidden_grad, query_grad, kv_grad, norm_dot.reshape(row_count))


def solution(mesh):
    placed = (
        P("seq", None),
        P(),
        P("seq", None, None),
        P(),
        P("section", "mp"),
        P(None, None, "mp"),
        P("seq", "mp"),
        P("seq", None),
        P("seq"),
    )
    return jax.shard_map(
        body,
        mesh=mesh,
        in_specs=placed,
        out_specs=(
            P("seq", ("section", "mp")),
            P(("section", "seq"), "mp"),
            P(None, ("section", "seq"), "mp"),
            P("seq"),
        ),
        check_vma=False,
    )
```
